32 devices in a mesh: ctx: 8 (over z, y), fsdp: 4 (over x, core).
Axes of the slice: x: 2, y: 2, z: 4, core: 2. Of those that a mesh axis runs over, the one named last changes fastest.
Arguments:
- tokens: bfloat16 [4, 1024, 2048], P('fsdp', 'ctx'), may hold values from -6 to 6
- teacher: bfloat16 [4, 1024, 2048], P('fsdp', 'ctx'), may hold values from -6 to 6
- valid_mask: int32 [4, 1024], P('fsdp', 'ctx'), may hold values 0 or 1
- lengths: int32 [4, 4], P('fsdp'), may hold values from 1 to 512, 1024 in all within a row
- span_order: int32 [4, 8], P('fsdp', 'ctx'), may hold values from 0 to 7, as said below
- w_query: bfloat16 [2048, 2048], P(('ctx', 'fsdp')), may hold values from -0.125 to 0.125
- w_key: bfloat16 [2048, 512], P(('ctx', 'fsdp')), may hold values from -0.125 to 0.125
- w_value: bfloat16 [2048, 512], P(('ctx', 'fsdp')), may hold values from -0.125 to 0.125
- w_out: bfloat16 [2048, 2048], P(('ctx', 'fsdp')), may hold values from -1 to 1
- w_gate: bfloat16 [2048, 8192], P(('ctx', 'fsdp')), may hold values from -0.125 to 0.125
- w_up: bfloat16 [2048, 8192], P(('ctx', 'fsdp')), may hold values from -0.125 to 0.125
- w_down: bfloat16 [8192, 2048], P(('ctx', 'fsdp')), may hold values from -0.0625 to 0.0625
- gain_attn: bfloat16 [2048], P(('ctx', 'fsdp')), may hold values from 0.099609375 to 1.8984375
- gain_ffn: bfloat16 [2048], P(('ctx', 'fsdp')), may hold values from 0.099609375 to 1.8984375
Outputs:
- output: bfloat16 [4, 1024, 2048], P('fsdp', 'ctx')
- loss_value: float32 [], replicated
- grad_tokens: float32 [4, 1024, 2048], P('fsdp', 'ctx')
- grad_w_query: float32 [2048, 2048], P(('ctx', 'fsdp'))
- grad_w_key: float32 [2048, 512], P(('ctx', 'fsdp'))
- grad_w_value: float32 [2048, 512], P(('ctx', 'fsdp'))
- grad_w_out: float32 [2048, 2048], P(('ctx', 'fsdp'))
- grad_w_gate: float32 [2048, 8192], P(('ctx', 'fsdp'))
- grad_w_up: float32 [2048, 8192], P(('ctx', 'fsdp'))
- grad_w_down: float32 [8192, 2048], P(('ctx', 'fsdp'))
- grad_gain_attn: float32 [2048], P(('ctx', 'fsdp'))
- grad_gain_ffn: float32 [2048], P(('ctx', 'fsdp'))
The draws below stay inside these ranges and needn't reach their ends.
Inputs may be any that keep to these rules, and one draw needn't show every extreme that they name: Each row lists the lengths of the 4 sequences of one stream in stream order; they sum to 1024 and the longest is exactly 512. `span_order`: each row is a permutation of the span numbers of one stream; entry c names the stream span held in token slots c * 128 to c * 128 + 127. The spans of one context device, in slot order, are r, r + 8, r + 16, ..., one residue r for each device.
All inputs are finite; a program needn't handle non-finite values. No bound on the sum of `valid_mask` on one device may be relied on, other than what follows from the above.
Results may differ from the reference program's by a relative error of at most 0.015.
Values may be sent and summed in bfloat16 or wider, within the bound.
No kernel may reach another device: no remote copies, remote signals or barrier semaphores. Data moves between devices by JAX's collectives and lax.ppermute only.
A program may use at most 576 MiB of HBM per device.

```python
import math
import jax
import jax.numpy as jnp
import numpy as np
from jax import lax

D = 2048
HEADS = 32
KV_HEADS = 8
HEAD_DIM = 64
FF = 8192
SPAN = 128
NSEQ = 4
TOK_DEV = 128
CYCLE = 8
STREAM = 1024
STREAMS = 4
TOKENS = 4096
SPANS = 8


def draw_span_order(key, part):
    key = jax.random.fold_in(key, 7)
    stream_keys = jax.random.split(key, STREAMS)
    per_device = TOK_DEV // SPAN

    def per_stream(stream_key):
        residues = jax.random.permutation(stream_key, jnp.arange(CYCLE, dtype=jnp.int32))
        local_index = jnp.arange(SPANS, dtype=jnp.int32)
        device = local_index // per_device
        band = local_index % per_device
        owner_residue = jnp.sum(jnp.where(jnp.arange(CYCLE, dtype=jnp.int32)[None, :] == device[:, None], residues[None, :], 0), axis=1)
        return (band * CYCLE + owner_residue).astype(jnp.int32)
    return jax.vmap(per_stream)(stream_keys).astype(jnp.int32)


def with_ends(drawn, key, smallest, top_value):
    longest = drawn.shape.index(max(drawn.shape))
    spots = []
    for shift in (0, 1):
        where = [jax.random.randint(jax.random.fold_in(key, axis), (), 0, length) for axis, length in enumerate(drawn.shape)]
        where[longest] = (where[longest] + shift) % drawn.shape[longest]
        spots.append(tuple(where))
    return drawn.at[spots[0]].set(smallest).at[spots[1]].set(top_value)


def block_levels(key, shape, cuts, low, largest):
    factor_of = 1.0
    for dim, shards_of in cuts:
        draws = jax.random.uniform(jax.random.fold_in(jax.random.fold_in(key, 6), dim), (shards_of,), jnp.float32, low / len(cuts), largest / len(cuts))
        factor_of = factor_of * jnp.repeat(jnp.exp(draws), shape[dim] // shards_of).reshape((-1,) + (1,) * (len(shape) - 1 - dim))
    return factor_of


def profile(amount, total, most, skew):
    weights = [(1 << 20) // math.isqrt(grade ** skew) + 1 for grade in range(2, amount + 1)]
    spare, holding = total - most - (amount - 1), [1] * (amount - 1)
    while spare > 0:
        movable = [i for i in range(amount - 1) if holding[i] < most]
        pool, left = sum([weights[i] for i in movable]), spare
        for i in movable:
            addition = min(most - holding[i], max(1, left * weights[i] // pool), spare)
            holding[i] = holding[i] + addition
            spare = spare - addition
    return np.array([most] + holding)


def ragged_sizes(key, number_of, total, limit, slope):
    if number_of == 2:
        one = jax.random.randint(key, (), max(1, total - limit), min(limit, total - 1) + 1)
        return jnp.stack([one, total - one])
    tallies = jnp.asarray(profile(number_of, total, limit, slope), jnp.int32)
    pairs = (number_of - 1) // 2
    giver, taker = tallies[1:1 + 2 * pairs:2], tallies[2:2 + 2 * pairs:2]
    slack = jnp.minimum(giver - 1, limit - taker)
    moved = jax.random.randint(jax.random.fold_in(key, 1), (pairs,), 0, 1 << 20) % (slack + 1)
    tallies = tallies.at[1:1 + 2 * pairs:2].set(giver - moved).at[2:2 + 2 * pairs:2].set(taker + moved)
    return tallies[jax.random.permutation(jax.random.fold_in(key, 2), number_of)]


def bell_draw(own_key, shape, width, limit, cuts=(), held_as=jnp.bfloat16):
    result = jax.random.normal(own_key, shape, jnp.float32) * width
    if len(cuts) > 0:
        result = block_levels(own_key, shape, cuts, -0.22, 0.18) * result
    return jnp.clip(result, min=-limit, max=limit).astype(held_as)


def setup_inputs(seed: int = 0) -> dict:
    splits = jax.random.split(jax.random.key(seed), 15)
    return {
        "tokens": bell_draw(splits[0], (STREAMS, STREAM, D), 1.0, 6.0, ((0, 4), (1, 8))),
        "teacher": bell_draw(splits[1], (STREAMS, STREAM, D), 1.0, 6.0, ((0, 4), (1, 8))),
        "valid_mask": with_ends((jax.random.randint(splits[2], (STREAMS, STREAM), 0, 4) < 3).astype(jnp.int32), jax.random.fold_in(splits[2], 1), 0, 1),
        "lengths": jax.vmap(lambda own: ragged_sizes(own, NSEQ, STREAM, STREAM // 2, 2))(jax.random.split(splits[3], STREAMS)).reshape((STREAMS, NSEQ)).astype(jnp.int32),
        "span_order": draw_span_order(jax.random.fold_in(splits[14], 71), 0),
        "w_query": bell_draw(splits[5], (D, D), D ** -0.5, 0.125, ((0, 32),)),
        "w_key": bell_draw(splits[6], (D, KV_HEADS * HEAD_DIM), D ** -0.5, 0.125, ((0, 32),)),
        "w_value": bell_draw(splits[7], (D, KV_HEADS * HEAD_DIM), D ** -0.5, 0.125, ((0, 32),)),
        "w_out": bell_draw(splits[8], (D, D), (D // 64) ** -0.5, 1.0, ((0, 32),)),
        "w_gate": bell_draw(splits[9], (D, FF), D ** -0.5, 0.125, ((0, 32),)),
        "w_up": bell_draw(splits[10], (D, FF), D ** -0.5, 0.125, ((0, 32),)),
        "w_down": bell_draw(splits[11], (FF, D), FF ** -0.5, 0.0625, ((0, 32),)),
        "gain_attn": jnp.clip(1.0 + 0.18 * jax.random.normal(splits[12], (D,), jnp.float32), 0.099609375, 1.8984375).astype(jnp.bfloat16),
        "gain_ffn": jnp.clip(1.0 + 0.18 * jax.random.normal(splits[13], (D,), jnp.float32), 0.099609375, 1.8984375).astype(jnp.bfloat16),
    }


@jax.custom_vjp
def low(v):
    return lax.optimization_barrier(v.astype(jnp.bfloat16)).astype(jnp.float32)

@jax.custom_vjp
def low_back(v):
    return v

def low_keep(v):
    return (low(v), None)

def low_pass(kept, grad):
    return (grad,)

def back_keep(v):
    return (v, None)

def back_low(kept, grad):
    return (low(grad),)
low.defvjp(low_keep, low_pass)
low_back.defvjp(back_keep, back_low)
EPSILON = 1e-05
HIGHEST = lax.Precision.HIGHEST

def rope_rates(head_width):
    frequency = 1.0 / 500000.0 ** (np.arange(0, head_width, 2) / head_width)
    wavelength = 2.0 * np.pi / frequency
    blend_share = (8192.0 / wavelength - 1.0) / 3.0
    blended = (1.0 - blend_share) * frequency / 32.0 + blend_share * frequency
    frequency = np.where(wavelength < 2048.0, frequency, np.where(wavelength > 8192.0, frequency / 32.0, blended))
    return np.concatenate([frequency, frequency]).astype(np.float32)

def rotate(values, angles):
    half_dim = values.shape[-1] // 2
    turned = jnp.concatenate([-values[..., half_dim:], values[..., :half_dim]], axis=-1)
    return values * jnp.cos(angles)[:, None, :] + turned * jnp.sin(angles)[:, None, :]

def stream_places(lengths_row, order_row):
    slot_index = jnp.arange(STREAM, dtype=jnp.int32)
    stream_place = (jnp.repeat(order_row, SPAN) * SPAN + slot_index % SPAN).astype(jnp.int32)
    seq_ends = jnp.cumsum(lengths_row).astype(jnp.int32)
    passed = seq_ends[None, :] <= stream_place[:, None]
    segment = lax.optimization_barrier(jnp.sum(passed.astype(jnp.int32), axis=1)).astype(jnp.int32)
    seq_begin = lax.optimization_barrier(jnp.sum(jnp.where(passed, lengths_row[None, :], 0), axis=1)).astype(jnp.int32)
    return (stream_place, segment, (stream_place - seq_begin).astype(jnp.int32))

def rms_norm(values, gain):
    inverse = lax.rsqrt(lax.optimization_barrier(jnp.mean(values * values, axis=1, keepdims=True)) + EPSILON)
    return values * inverse * gain

def stream_forward(inputs, teacher_row, valid_row, stream_place, segment, position, weights):
    w_query, w_key, w_value, w_out, w_gate, w_up, w_down, gain_attn, gain_ffn = weights
    group_size = HEADS // KV_HEADS
    score_scale = 1.0 / math.sqrt(HEAD_DIM)
    angles = position.astype(jnp.float32)[:, None] * jnp.asarray(rope_rates(HEAD_DIM))[None, :]
    normed_attn = low(rms_norm(inputs, gain_attn))
    query_act = low_back(jnp.dot(normed_attn, w_query, precision=HIGHEST))
    key_act = low_back(jnp.dot(normed_attn, w_key, precision=HIGHEST))
    value_rows = low(low_back(jnp.dot(normed_attn, w_value, precision=HIGHEST)))
    query_rows = low(rotate(query_act.reshape(STREAM, HEADS, HEAD_DIM), angles))
    key_rows = low(rotate(key_act.reshape(STREAM, KV_HEADS, HEAD_DIM), angles))
    value_rows = value_rows.reshape(STREAM, KV_HEADS, HEAD_DIM)
    block_rows = math.gcd(512, STREAM)
    block_count = STREAM // block_rows

    @jax.checkpoint
    def attend(block_items):
        query_block, place_block, seg_block = block_items
        grouped = query_block.reshape(block_rows, KV_HEADS, group_size, HEAD_DIM)
        raw_scores = low_back(jnp.einsum('qgrd,kgd->qgrk', grouped, key_rows, precision=HIGHEST))
        scores = raw_scores * score_scale
        visible = (seg_block[:, None] == segment[None, :]) & (stream_place[None, :] <= place_block[:, None])
        scores = jnp.where(visible[:, None, None, :], scores, -jnp.inf)
        row_max = lax.optimization_barrier(jnp.max(scores, axis=-1, keepdims=True))
        expo = jnp.exp(scores - row_max)
        probs = low(expo / lax.optimization_barrier(jnp.sum(expo, axis=-1, keepdims=True)))
        mixed_heads = jnp.einsum('qgrk,kgd->qgrd', probs, value_rows, precision=HIGHEST)
        return mixed_heads.reshape(block_rows, HEADS * HEAD_DIM)
    mixed_all = lax.map(attend, (query_rows.reshape(block_count, block_rows, HEADS, HEAD_DIM), stream_place.reshape(block_count, block_rows), segment.reshape(block_count, block_rows)))
    attended = low(low_back(mixed_all.reshape(STREAM, HEADS * HEAD_DIM)))
    middle = inputs + low_back(jnp.dot(attended, w_out, precision=HIGHEST))
    normed_ffn = low(rms_norm(middle, gain_ffn))
    gate_act = low_back(jnp.dot(normed_ffn, w_gate, precision=HIGHEST))
    up_act = low_back(jnp.dot(normed_ffn, w_up, precision=HIGHEST))
    hidden = low(jax.nn.silu(gate_act) * up_act)
    output = middle + low_back(jnp.dot(hidden, w_down, precision=HIGHEST))
    missed = (output - teacher_row) * valid_row[:, None]
    return (output, jnp.sum(missed * missed))

def reference(tokens, teacher, valid_mask, lengths, span_order, w_query, w_key, w_value, w_out, w_gate, w_up, w_down, gain_attn, gain_ffn):
    places, segments, positions = jax.vmap(stream_places)(lengths, span_order)
    valid_f = valid_mask.astype(jnp.float32)
    valid_count = jnp.sum(valid_f)
    spread = TOKENS / valid_count
    teacher_f = teacher.astype(jnp.float32)

    def objective(inputs_all, *weights):

        def per_stream(running, stream_items):
            inputs, teacher_row, valid_row, stream_place, segment, position = stream_items
            output, squares = stream_forward(inputs, teacher_row, valid_row, stream_place, segment, position, weights)
            return (running + squares, output)
        running, outputs = lax.scan(per_stream, jnp.zeros((), jnp.float32), (inputs_all, teacher_f, valid_f, places, segments, positions))
        return (0.5 * spread * running, (outputs, running))
    weights_f = tuple((weight.astype(jnp.float32) for weight in (w_query, w_key, w_value, w_out, w_gate, w_up, w_down, gain_attn, gain_ffn)))
    target, pull, extras = jax.vjp(objective, tokens.astype(jnp.float32), *weights_f, has_aux=True)
    outputs, running = extras
    gradients = pull(jnp.ones_like(target))
    loss_value = 0.5 * running / (D * valid_count)
    return (outputs.astype(jnp.bfloat16), loss_value, gradients[0], gradients[1], gradients[2], gradients[3], gradients[4], gradients[5], gradients[6], gradients[7], gradients[8], gradients[9])
```

```python
import functools
import math

import jax
import jax.numpy as jnp
import numpy as np
from jax import lax
from jax.experimental import pallas as pl
from jax.experimental.pallas import tpu as pltpu
from jax.sharding import PartitionSpec as P

HEADS = 32
KV_HEADS = 8
HEAD_DIM = 64
SPAN = 128
EPSILON = 1e-05
HIDE = -1e30
BF = jnp.bfloat16
F32 = jnp.float32


def rope_rates(head_width):
    frequency = 1.0 / 500000.0 ** (np.arange(0, head_width, 2) / head_width)
    wavelength = 2.0 * np.pi / frequency
    blend_share = (8192.0 / wavelength - 1.0) / 3.0
    blended = (1.0 - blend_share) * frequency / 32.0 + blend_share * frequency
    frequency = np.where(
        wavelength < 2048.0, frequency, np.where(wavelength > 8192.0, frequency / 32.0, blended)
    )
    return np.concatenate([frequency, frequency]).astype(np.float32)


def turn_matrix(heads):
    half = HEAD_DIM // 2
    one = np.zeros((HEAD_DIM, HEAD_DIM), np.float32)
    for i in range(half):
        one[i + half, i] = -1.0
        one[i, i + half] = 1.0
    return np.kron(np.eye(heads, dtype=np.float32), one)


def mm(left, right):
    return jnp.dot(left, right, preferred_element_type=F32)


def mm_t(left, right):
    return lax.dot_general(left, right, (((0,), (0,)), ((), ())), preferred_element_type=F32)


def against(left, right):
    return lax.dot_general(left, right, (((1,), (1,)), ((), ())), preferred_element_type=F32)


def pick(array, index, axis=0):
    return lax.dynamic_index_in_dim(array, index, axis, keepdims=False)


class Links:
    def __init__(self):
        self.n = lax.axis_size("ctx")
        self.m = lax.axis_size("fsdp")
        self.ring = self.n // 2
        self.c = lax.axis_index("ctx")
        self.f = lax.axis_index("fsdp")
        self.a = self.c // 2
        self.b = self.c % 2

    def shift(self, x, da, dq):
        perm = [
            (a * 2 + b, ((a + da) % self.ring) * 2 + (b ^ dq))
            for a in range(self.ring)
            for b in range(2)
        ]
        return lax.ppermute(x, "ctx", perm)

    def flip(self, x, axis, bit):
        size = self.n if axis == "ctx" else self.m
        return lax.ppermute(x, axis, [(i, i ^ bit) for i in range(size)])

    def total(self, x, axes):
        for axis in axes:
            bit = 1
            while bit < (self.n if axis == "ctx" else self.m):
                x = x + self.flip(x, axis, bit)
                bit *= 2
        return x

    def gather_ctx(self, x):
        out = []
        for r in range(self.ring):
            if r:
                x = self.shift(x, 1, 0)
            out.append((x, self.shift(x, 0, 1)))
        return out

    def scatter_order(self):
        return list(range(1, self.ring)) + [0]

    def scatter_ctx(self, part):
        held = None
        for r in self.scatter_order():
            mine, other = part(r)
            term = mine + self.shift(other.astype(BF), 0, 1).astype(F32)
            if held is not None:
                term = term + self.shift(held.astype(BF), 1, 0).astype(F32)
            held = term
        return held

    def exchange_ctx(self, pieces):
        out = pieces
        zeros = (0,) * (pieces.ndim - 1)
        for da in range(self.ring):
            for dq in range(2):
                if da == 0 and dq == 0:
                    continue
                dest = ((self.a + da) % self.ring) * 2 + (self.b ^ dq)
                src = ((self.a + self.ring - da) % self.ring) * 2 + (self.b ^ dq)
                got = self.shift(pick(pieces, dest), da, dq)
                out = lax.dynamic_update_slice(out, got[None], (src,) + zeros)
        return out

    def gather_fsdp(self, x, axis):
        held = [(0, x)]
        bit = self.m // 2
        while bit:
            held = held + [(mark | bit, self.flip(block, "fsdp", bit)) for mark, block in held]
            bit //= 2
        shape = x.shape[:axis] + (self.m,) + x.shape[axis:]
        out = jnp.zeros(shape, x.dtype)
        for mark, block in held:
            start = [0] * len(shape)
            start[axis] = self.f ^ mark
            out = lax.dynamic_update_slice(out, jnp.expand_dims(block, axis), tuple(start))
        return out

    def scatter_fsdp(self, x, axis):
        bit = 1
        while bit < self.m:
            mine = (self.f // bit) % 2
            shape = x.shape[:axis] + (x.shape[axis] // 2, 2) + x.shape[axis + 1 :]
            x = x.reshape(shape)
            sent = self.flip(pick(x, 1 - mine, axis + 1).astype(BF), "fsdp", bit)
            x = pick(x, mine, axis + 1) + sent.astype(F32)
            bit *= 2
        return lax.squeeze(x, (axis,))


def attend_kernel(heads, q_ref, k_ref, v_ref, info_q, info_k, o_ref, lse_ref, kpad, vpad):
    width = heads * HEAD_DIM
    head_of = lax.broadcasted_iota(jnp.int32, (1, width), 1) // HEAD_DIM

    @pl.when(pl.program_id(0) == 0)
    def _():
        for h in range(heads):
            kpad[h] = jnp.where(head_of == h, k_ref[...], 0).astype(BF)
            vpad[h] = jnp.where(head_of == h, v_ref[...], 0).astype(BF)

    seen = (info_q[:, 0:1] == info_k[0:1, :]) & (info_k[1:2, :] <= info_q[:, 1:2])
    bias = jnp.where(seen, 0.0, HIDE)
    lane = lax.broadcasted_iota(jnp.int32, (1, 128), 1)
    q = q_ref[...]
    out = jnp.zeros((q.shape[0], width), F32)
    lse = jnp.zeros((q.shape[0], 128), F32)
    for h in range(heads):
        s = against(q, kpad[h]) + bias
        top = jnp.max(s, axis=1, keepdims=True)
        p = jnp.exp(s - top)
        total = jnp.sum(p, axis=1, keepdims=True)
        out = out + mm(p.astype(BF), vpad[h]) / total
        lse = jnp.where(lane == h, top + jnp.log(total), lse)
    o_ref[...] = out.astype(BF)
    lse_ref[...] = lse


def attend_back_kernel(
    heads, q_ref, g_ref, k_ref, v_ref, info_q, info_k, lse_ref,
    dq_ref, dk_ref, dv_ref, kpad, vpad,
):
    width = heads * HEAD_DIM
    head_of = lax.broadcasted_iota(jnp.int32, (1, width), 1) // HEAD_DIM

    @pl.when(pl.program_id(0) == 0)
    def _():
        for h in range(heads):
            kpad[h] = jnp.where(head_of == h, k_ref[...], 0).astype(BF)
            vpad[h] = jnp.where(head_of == h, v_ref[...], 0).astype(BF)
        dk_ref[...] = jnp.zeros_like(dk_ref)
        dv_ref[...] = jnp.zeros_like(dv_ref)

    seen = (info_q[:, 0:1] == info_k[0:1, :]) & (info_k[1:2, :] <= info_q[:, 1:2])
    bias = jnp.where(seen, 0.0, HIDE)
    q = q_ref[...]
    g = g_ref[...]
    dq = jnp.zeros((q.shape[0], width), F32)
    for h in range(heads):
        p = jnp.exp(against(q, kpad[h]) + (bias - lse_ref[:, h : h + 1]))
        dp = against(g, vpad[h])
        delta = jnp.sum(p * dp, axis=1, keepdims=True)
        ds = (p * (dp - delta)).astype(BF)
        dq = dq + mm(ds, kpad[h])
        own = head_of == h
        dk_ref[...] += mm_t(ds, jnp.where(own, q, 0).astype(BF))
        dv_ref[...] += mm_t(p.astype(BF), jnp.where(own, g, 0).astype(BF))
    dq_ref[...] = dq * (1.0 / math.sqrt(HEAD_DIM))


def attend_specs(rows, stream, width):
    by_row = pl.BlockSpec((rows, width), lambda i: (i, 0))
    whole = pl.BlockSpec((stream, width), lambda i: (0, 0))
    mark = pl.BlockSpec((rows, 128), lambda i: (i, 0))
    marks = pl.BlockSpec((8, stream), lambda i: (0, 0))
    return by_row, whole, mark, marks


def attend(heads, q, k, v, info_q, info_k):
    stream, width = q.shape
    rows = 256 if stream <= 1024 else 128
    by_row, whole, mark, marks = attend_specs(rows, stream, width)
    return pl.pallas_call(
        functools.partial(attend_kernel, heads),
        grid=(stream // rows,),
        in_specs=[by_row, whole, whole, mark, marks],
        out_specs=[by_row, mark],
        out_shape=[
            jax.ShapeDtypeStruct((stream, width), BF),
            jax.ShapeDtypeStruct((stream, 128), F32),
        ],
        scratch_shapes=[pltpu.VMEM((heads, stream, width), BF)] * 2,
        compiler_params=pltpu.CompilerParams(vmem_limit_bytes=40 << 20),
        cost_estimate=pl.CostEstimate(
            flops=4 * stream * stream * heads * 256,
            bytes_accessed=8 * stream * width,
            transcendentals=stream * stream * heads,
        ),
    )(q, k, v, info_q, info_k)


def attend_back(heads, q, g, k, v, info_q, info_k, lse):
    stream, width = q.shape
    rows = 256 if stream <= 1024 else 128
    by_row, whole, mark, marks = attend_specs(rows, stream, width)
    return pl.pallas_call(
        functools.partial(attend_back_kernel, heads),
        grid=(stream // rows,),
        in_specs=[by_row, by_row, whole, whole, mark, marks, mark],
        out_specs=[by_row, whole, whole],
        out_shape=[jax.ShapeDtypeStruct((stream, width), F32)] * 3,
        scratch_shapes=[pltpu.VMEM((heads, stream, width), BF)] * 2,
        compiler_params=pltpu.CompilerParams(vmem_limit_bytes=40 << 20),
        cost_estimate=pl.CostEstimate(
            flops=10 * stream * stream * heads * 256,
            bytes_accessed=20 * stream * width,
            transcendentals=stream * stream * heads,
        ),
    )(q, g, k, v, info_q, info_k, lse)


def norm_back(grad_scaled, unit_rows, inverse):
    return inverse * (
        grad_scaled - unit_rows * jnp.mean(grad_scaled * unit_rows, axis=1, keepdims=True)
    )


def rms_inverse(values):
    return lax.rsqrt(jnp.mean(values * values, axis=1, keepdims=True) + EPSILON)


def body(
    tokens,
    teacher,
    valid_mask,
    lengths,
    span_order,
    w_query,
    w_key,
    w_value,
    w_out,
    w_gate,
    w_up,
    w_down,
    gain_attn,
    gain_ffn,
):
    net = Links()
    n, m, ring = net.n, net.m, net.ring
    x_low = tokens[0]
    tok_rows, width = x_low.shape
    rows = w_query.shape[0]
    heads = HEADS // n
    q_width = heads * HEAD_DIM
    sharers = n // KV_HEADS
    ff_slice = w_gate.shape[1] // n
    stream = tok_rows * n
    spans = tok_rows // SPAN

    own_spans = jnp.where(
        lax.broadcasted_iota(jnp.int32, (n, spans), 0) == net.c, span_order[0][None, :], 0
    ).reshape(1, n * spans)
    own_count = jnp.sum(valid_mask).astype(jnp.int32).reshape(1, 1)
    small = net.total(jnp.concatenate([own_spans, own_count], axis=1), ["ctx"])
    order_all = small[0, : n * spans].reshape(n, spans)
    valid_count = net.total(small[:, n * spans :], ["fsdp"])[0, 0].astype(F32)

    token_blocks = net.gather_ctx(x_low)
    gain_a = gain_attn.astype(F32)[:, None]
    gain_f = gain_ffn.astype(F32)[:, None]

    def folded(weight, gain):
        return (weight.astype(F32) * gain).astype(BF)

    def by_slice(weight, count):
        return jnp.swapaxes(weight.reshape(rows, count, weight.shape[1] // count), 0, 1)

    def kv_slices(weight):
        return jnp.repeat(by_slice(weight, KV_HEADS), sharers, axis=0)

    qkv_pieces = jnp.concatenate(
        [
            by_slice(folded(w_query, gain_a), n),
            kv_slices(folded(w_key, gain_a)),
            kv_slices(folded(w_value, gain_a)),
        ],
        axis=2,
    )
    qkv_w = net.gather_fsdp(net.exchange_ctx(qkv_pieces), 1).reshape(width, q_width + 2 * HEAD_DIM)
    wq = qkv_w[:, :q_width]
    wk = jnp.tile(qkv_w[:, q_width : q_width + HEAD_DIM], (1, heads))
    wv = jnp.tile(qkv_w[:, q_width + HEAD_DIM :], (1, heads))
    turn = jnp.asarray(turn_matrix(2 * heads), BF)
    w_lin = jnp.concatenate([wq, wk, wv], axis=1)
    w_turn = mm(w_lin[:, : 2 * q_width], turn).astype(BF)
    w_attn = jnp.concatenate([w_lin, w_turn], axis=1)
    out_w = net.gather_fsdp(w_out, 0).reshape(q_width, width)

    def slot_source(r, q):
        return ((net.a + ring - r) % ring) * 2 + (net.b ^ q)

    spans_here = jnp.concatenate(
        [pick(order_all, slot_source(r, q)) for r in range(ring) for q in range(2)]
    )
    place = (
        spans_here[:, None] * SPAN + lax.broadcasted_iota(jnp.int32, (n * spans, SPAN), 1)
    ).reshape(stream)
    seq_ends = jnp.cumsum(lengths[0])
    passed = seq_ends[None, :] <= place[:, None]
    segment = jnp.sum(passed.astype(jnp.int32), axis=1)
    seq_begin = jnp.sum(jnp.where(passed, lengths[0][None, :], 0), axis=1)
    rates = jnp.asarray(rope_rates(HEAD_DIM)[: HEAD_DIM // 2])
    angles = (place - seq_begin).astype(F32)[:, None] * rates[None, :]
    cosines = jnp.tile(jnp.cos(angles), (1, 2 * 2 * heads))
    sines = jnp.tile(jnp.sin(angles), (1, 2 * 2 * heads))
    info_q = jnp.pad(jnp.stack([segment, place], axis=1), ((0, 0), (0, 126)))
    info_k = jnp.pad(jnp.stack([segment, place], axis=0), ((0, 6), (0, 0)))
    score_scale = 1.0 / math.sqrt(HEAD_DIM)

    x_all, inverse_all, q_all, k_all, v_all = [], [], [], [], []
    pair_rows = 2 * tok_rows
    for r in range(ring):
        x_pair = jnp.concatenate(token_blocks[r], axis=0)
        inverse = rms_inverse(x_pair.astype(F32))
        act = mm(x_pair, w_attn)
        cos_r = cosines[r * pair_rows : (r + 1) * pair_rows]
        sin_r = sines[r * pair_rows : (r + 1) * pair_rows]
        rot = (act[:, : 2 * q_width] * cos_r + act[:, 3 * q_width :] * sin_r) * inverse
        x_all.append(x_pair)
        inverse_all.append(inverse)
        q_all.append((rot[:, :q_width] * score_scale).astype(BF))
        k_all.append(rot[:, q_width:].astype(BF))
        v_all.append((act[:, 2 * q_width : 3 * q_width] * inverse).astype(BF))
    x_all = jnp.concatenate(x_all, axis=0)
    inverse_all = jnp.concatenate(inverse_all, axis=0)
    q_all = jnp.concatenate(q_all, axis=0)
    k_all = jnp.concatenate(k_all, axis=0)
    v_all = jnp.concatenate(v_all, axis=0)
    attended, lse = attend(heads, q_all, k_all, v_all, info_q, info_k)

    def split_pair(block):
        return block[:tok_rows], block[tok_rows:]

    def pair_of(array, r):
        return array[r * pair_rows : (r + 1) * pair_rows]

    inputs = x_low.astype(F32)
    middle = inputs + net.scatter_ctx(lambda r: split_pair(mm(pair_of(attended, r), out_w)))

    gate_up_pieces = jnp.concatenate(
        [by_slice(folded(w_gate, gain_f), n), by_slice(folded(w_up, gain_f), n)], axis=2
    )
    gate_up_w = net.gather_fsdp(net.exchange_ctx(gate_up_pieces), 1).reshape(width, 2 * ff_slice)
    down_w = net.gather_fsdp(w_down, 0).reshape(ff_slice, width)

    inverse_ffn = rms_inverse(middle)
    unit_ffn = middle * inverse_ffn
    unit_blocks = net.gather_ctx(unit_ffn.astype(BF))
    z_pairs = [jnp.concatenate(blocks, axis=0) for blocks in unit_blocks]
    acts, hiddens = {}, {}

    def down_part(r):
        both = mm(z_pairs[r], gate_up_w)
        gate, up = both[:, :ff_slice], both[:, ff_slice:]
        acts[r] = (gate, up)
        hiddens[r] = (gate * jax.nn.sigmoid(gate) * up).astype(BF)
        return split_pair(mm(hiddens[r], down_w))

    out_full = middle + net.scatter_ctx(down_part)

    valid_f = valid_mask[0].astype(F32)[:, None]
    missed = (out_full - teacher[0].astype(F32)) * valid_f
    square_sum = net.total(jnp.sum(missed * missed).reshape(1, 1), ["ctx", "fsdp"])[0, 0]
    loss_value = 0.5 * square_sum / (width * valid_count)
    grad_out = missed * ((tok_rows * n * m) / valid_count)

    grad_blocks = net.gather_ctx(grad_out.astype(BF))
    grad_pairs = [jnp.concatenate(blocks, axis=0) for blocks in grad_blocks]
    grad_acts = {}

    def unit_part(r):
        gate, up = acts[r]
        grad_hidden = against(grad_pairs[r], down_w)
        share = jax.nn.sigmoid(gate)
        grad_gate = grad_hidden * up * share * (1.0 + gate * (1.0 - share))
        grad_up = grad_hidden * (gate * share)
        grad_acts[r] = jnp.concatenate([grad_gate.astype(BF), grad_up.astype(BF)], axis=1)
        return split_pair(against(grad_acts[r], gate_up_w))

    grad_unit = net.scatter_ctx(unit_part)
    grad_middle = grad_out + norm_back(grad_unit, unit_ffn, inverse_ffn)
    middle_low = grad_middle.astype(BF)

    def joined(items):
        return jnp.concatenate([items[r] for r in range(ring)], axis=0)

    down_term = mm_t(joined(hiddens), joined(grad_pairs))
    gate_up_term = mm_t(joined(z_pairs), joined(grad_acts))
    grad_down = net.scatter_fsdp(down_term.reshape(m, ff_slice // m, width), 0)
    gate_up_mine = net.exchange_ctx(
        net.scatter_fsdp(gate_up_term.reshape(n, m, rows, 2 * ff_slice), 1).astype(BF)
    ).astype(F32)

    middle_pairs = [jnp.concatenate(blocks, axis=0) for blocks in net.gather_ctx(middle_low)]
    grad_attended = jnp.concatenate(
        [against(pair, out_w).astype(BF) for pair in middle_pairs], axis=0
    )
    grad_q, grad_k, grad_v = attend_back(
        heads, q_all, grad_attended, k_all, v_all, info_q, info_k, lse
    )
    grad_rot = jnp.concatenate([grad_q, grad_k], axis=1)
    sined = grad_rot * sines
    sined_high = sined.astype(BF)
    sined_low = (sined - sined_high.astype(F32)).astype(BF)
    turned = against(sined_high, turn) + against(sined_low, turn)
    grad_act = jnp.concatenate([grad_rot * cosines + turned, grad_v], axis=1)
    grad_act_low = grad_act.astype(BF)
    grad_attn = net.scatter_ctx(lambda r: split_pair(against(pair_of(grad_act_low, r), w_lin)))
    inverse_attn = rms_inverse(inputs)
    grad_input = grad_middle + norm_back(grad_attn, inputs * inverse_attn, inverse_attn)

    qkv_term = mm_t(x_all, (grad_act * inverse_all).astype(BF))

    def fold(block):
        return jnp.sum(block.reshape(width, heads, HEAD_DIM), axis=1)

    qkv_term = jnp.concatenate(
        [
            qkv_term[:, :q_width],
            fold(qkv_term[:, q_width : 2 * q_width]),
            fold(qkv_term[:, 2 * q_width :]),
        ],
        axis=1,
    )
    qkv_mine = net.exchange_ctx(
        net.scatter_fsdp(qkv_term.reshape(n, m, rows, q_width + 2 * HEAD_DIM), 1).astype(BF)
    ).astype(F32)
    out_term = mm_t(attended, joined(middle_pairs))
    grad_w_out = net.scatter_fsdp(out_term.reshape(m, rows, width), 0)

    def laid(pieces):
        return jnp.swapaxes(pieces, 0, 1).reshape(rows, pieces.shape[0] * pieces.shape[2])

    def kv_laid(pieces):
        return laid(jnp.sum(pieces.reshape(KV_HEADS, sharers, rows, HEAD_DIM), axis=1))

    raw_q = laid(qkv_mine[:, :, :q_width])
    raw_k = kv_laid(qkv_mine[:, :, q_width : q_width + HEAD_DIM])
    raw_v = kv_laid(qkv_mine[:, :, q_width + HEAD_DIM :])
    raw_gate = laid(gate_up_mine[:, :, :ff_slice])
    raw_up = laid(gate_up_mine[:, :, ff_slice:])

    def gain_sum(pairs):
        return sum(jnp.sum(w.astype(F32) * g, axis=1) for w, g in pairs)

    grad_gain_attn = gain_sum([(w_query, raw_q), (w_key, raw_k), (w_value, raw_v)])
    grad_gain_ffn = gain_sum([(w_gate, raw_gate), (w_up, raw_up)])
    return (
        out_full.astype(BF)[None],
        loss_value,
        grad_input[None],
        raw_q * gain_a,
        raw_k * gain_a,
        raw_v * gain_a,
        grad_w_out,
        raw_gate * gain_f,
        raw_up * gain_f,
        grad_down,
        grad_gain_attn,
        grad_gain_ffn,
    )


def solution(mesh):
    token_spec = P("fsdp", "ctx", None)
    row_spec = P(("ctx", "fsdp"), None)
    gain_spec = P(("ctx", "fsdp"))
    in_specs = (
        token_spec,
        token_spec,
        P("fsdp", "ctx"),
        P("fsdp", None),
        P("fsdp", "ctx"),
        *([row_spec] * 7),
        gain_spec,
        gain_spec,
    )
    out_specs = (token_spec, P(), token_spec, *([row_spec] * 7), gain_spec, gain_spec)
    return jax.shard_map(body, mesh=mesh, in_specs=in_specs, out_specs=out_specs, check_vma=False)
```

```python
import functools
import math

import jax
import jax.numpy as jnp
import numpy as np
from jax import lax
from jax.experimental import pallas as pl
from jax.experimental.pallas import tpu as pltpu
from jax.sharding import PartitionSpec as P

HEADS = 32
KV_HEADS = 8
HEAD_DIM = 64
SPAN = 128
EPSILON = 1e-05
HIDE = -1e30
TWICE = ("bf", "bo")
BF = jnp.bfloat16
F32 = jnp.float32


def rope_rates(head_width):
    frequency = 1.0 / 500000.0 ** (np.arange(0, head_width, 2) / head_width)
    wavelength = 2.0 * np.pi / frequency
    blend_share = (8192.0 / wavelength - 1.0) / 3.0
    blended = (1.0 - blend_share) * frequency / 32.0 + blend_share * frequency
    frequency = np.where(
        wavelength < 2048.0, frequency, np.where(wavelength > 8192.0, frequency / 32.0, blended)
    )
    return np.concatenate([frequency, frequency]).astype(np.float32)


def mm(left, right):
    return jnp.dot(left, right, preferred_element_type=F32)


def mm_t(left, right):
    return lax.dot_general(left, right, (((0,), (0,)), ((), ())), preferred_element_type=F32)


def against(left, right):
    return lax.dot_general(left, right, (((1,), (1,)), ((), ())), preferred_element_type=F32)


def pick(array, index, axis=0):
    return lax.dynamic_index_in_dim(array, index, axis, keepdims=False)


def paired(blocks):
    rows = [jnp.concatenate(pieces, axis=1) if len(pieces) > 1 else pieces[0] for pieces in blocks]
    return jnp.concatenate(rows, axis=0)


def tie(value, *others):
    return lax.optimization_barrier((value, *others))[0]


class Links:
    def __init__(self):
        self.n = lax.axis_size("ctx")
        self.m = lax.axis_size("fsdp")
        self.ring = self.n // 2
        self.c = lax.axis_index("ctx")
        self.f = lax.axis_index("fsdp")
        self.a = self.c // 2
        self.b = self.c % 2
        self.box, self.jobs = {}, {}

    def shift(self, x, da, dq):
        perm = [
            (a * 2 + b, ((a + da) % self.ring) * 2 + (b ^ dq))
            for a in range(self.ring)
            for b in range(2)
        ]
        return lax.ppermute(x, "ctx", perm)

    def flip(self, x, axis, bit):
        size = self.n if axis == "ctx" else self.m
        return lax.ppermute(x, axis, [(i, i ^ bit) for i in range(size)])

    def slot(self, name, begun, mains):
        made = {key: job(begun) for key, job in self.jobs.pop(name, {}).items()}
        mains, made = lax.optimization_barrier((mains, made))
        self.box.update(made)
        return mains

    def cut(self, x, name):
        count = 2 if name in TWICE else 1
        step = x.shape[1] // count
        return [x[:, i * step : (i + 1) * step] for i in range(count)]

    def gather_ctx(self, x, name):
        out = []
        held = self.cut(x, name)
        for r in range(self.ring):
            pairs, moved = [], []
            for i, piece in enumerate(held):
                mains = [self.shift(piece, 0, 1)]
                if r < self.ring - 1:
                    mains.append(self.shift(piece, 1, 0))
                last = i == len(held) - 1
                mains = self.slot(f"{name}{r}" if last else "", piece, mains)
                pairs.append(mains[0])
                moved.append(mains[-1])
            out.append((held, pairs))
            held = moved
        return out

    def scatter_order(self):
        return list(range(1, self.ring)) + [0]

    def scatter_ctx(self, part, name):
        count = len(self.cut(jnp.zeros((1, 2)), name))
        held, got = [None] * count, [None] * count
        for i, r in enumerate(self.scatter_order()):
            mine, other = part(r)
            pieces = zip(self.cut(mine, name), self.cut(other.astype(BF), name))
            for k, (own, away) in enumerate(pieces):
                if i:
                    away = tie(away, got[k])
                mains = [self.shift(away, 0, 1)]
                if i:
                    mains.append(self.shift(held[k].astype(BF), 1, 0))
                mains = self.slot(f"{name}{i}" if k == count - 1 else "", away, mains)
                got[k] = mains[0]
                held[k] = own + sum(block.astype(F32) for block in mains)
        return held[0] if count == 1 else jnp.concatenate(held, axis=1)

    def direct(self):
        near = sorted(range(1, self.ring), key=lambda da: (min(da, self.ring - da), da))
        return [(0, 0)] + [(da, 0) for da in near] + [(0, 1)] + [(da, 1) for da in near]

    def dests(self, moves):
        spots = [((self.a + da) % self.ring) * 2 + (self.b ^ dq) for da, dq in moves]
        return jnp.stack(spots).astype(jnp.int32)

    def sources(self, moves):
        return self.dests([((self.ring - da) % self.ring, dq) for da, dq in moves])

    def routes(self):
        c = jnp.arange(self.n, dtype=jnp.int32)
        return ((c // 2 + self.ring - self.a) % self.ring) * 2 + (self.b ^ (c % 2))

    def origins(self):
        c = jnp.arange(self.n, dtype=jnp.int32)
        return ((self.a + self.ring - c // 2) % self.ring) * 2 + (self.b ^ (c % 2))

    def assemble(self, groups, spots, rows):
        sizes = [group[0].shape[0] for group in groups]
        count = sum(sizes)
        held_rows, width = groups[0][0].shape[1:]
        parts = max(1, min(width // 256, 8 // count))
        part = width // parts
        marks = self.f ^ jnp.arange(self.m, dtype=jnp.int32)
        specs, base = [], 0
        for size in sizes:

            def at(i, j, spots, base=base, size=size):
                return jnp.clip(i - base, 0, size - 1), 0, j

            specs += [pl.BlockSpec((1, held_rows, part), at)] * self.m
            base += size
        out = pl.pallas_call(
            functools.partial(place_kernel, sizes, self.m),
            grid_spec=pltpu.PrefetchScalarGridSpec(
                num_scalar_prefetch=1,
                grid=(count, parts),
                in_specs=specs,
                out_specs=pl.BlockSpec(
                    (1, self.m, rows, part), lambda i, j, spots: (spots[i], 0, 0, j)
                ),
            ),
            out_shape=jax.ShapeDtypeStruct((count, self.m, rows, width), BF),
            compiler_params=pltpu.CompilerParams(vmem_limit_bytes=24 << 20),
            cost_estimate=pl.CostEstimate(
                flops=0, bytes_accessed=4 * count * self.m * rows * width, transcendentals=0
            ),
        )(jnp.concatenate([spots, marks]), *[block for group in groups for block in group])
        return out.reshape(count * self.m * rows, width)


def place_kernel(sizes, m, spots, *refs):
    count = sum(sizes)
    out = refs[-1]
    base = 0
    for g, size in enumerate(sizes):

        @pl.when((pl.program_id(0) >= base) & (pl.program_id(0) < base + size))
        def _(g=g):
            for k in range(m):
                out[0, spots[count + k]] = refs[g * m + k][0, : out.shape[2]]

        base += size


def cut_qkv_kernel(n, spots, q_ref, k_ref, v_ref, gain_ref, span_ref, straight, across):
    rows = q_ref.shape[0]
    q_width = q_ref.shape[1] // n
    sharers = n // KV_HEADS
    gain = gain_ref[...]

    def folded(ref, i, width):
        return (ref[:, i * width : (i + 1) * width].astype(F32) * gain).astype(BF)

    for c in range(n):
        kv = c // sharers
        piece = jnp.concatenate(
            [
                folded(q_ref, c, q_width),
                folded(k_ref, kv, HEAD_DIM),
                folded(v_ref, kv, HEAD_DIM),
            ],
            axis=1,
        )
        move = spots[c]

        def fill(ref, piece=piece, move=move):
            ref[move // 2, :rows, :] = piece
            ref[move // 2, rows:, :] = jnp.broadcast_to(
                span_ref[0:16, : piece.shape[1]], (16, piece.shape[1])
            )

        pl.when(move % 2 == 0)(functools.partial(fill, straight))
        pl.when(move % 2 == 1)(functools.partial(fill, across))


def cut_qkv(n, spots, w_query, w_key, w_value, gain, span):
    rows = w_query.shape[0]
    width = w_query.shape[1] // n + 2 * HEAD_DIM
    vmem = pl.BlockSpec(memory_space=pltpu.VMEM)
    return pl.pallas_call(
        functools.partial(cut_qkv_kernel, n),
        in_specs=[pl.BlockSpec(memory_space=pltpu.SMEM)] + [vmem] * 5,
        out_specs=[vmem] * 2,
        out_shape=[jax.ShapeDtypeStruct((n // 2, rows + 16, width), BF)] * 2,
    )(spots, w_query, w_key, w_value, gain, span)


def cut_ffn_kernel(spots, gate, up, gain_ref, out):
    gain = gain_ref[...]
    width = gate.shape[1]
    out[0, :, :width] = (gate[...].astype(F32) * gain).astype(BF)
    out[0, :, width:] = (up[...].astype(F32) * gain).astype(BF)


def cut_ffn(dests, w_gate, w_up, gain):
    n = dests.shape[0]
    rows, width = w_gate.shape[0], w_gate.shape[1] // n
    block = pl.BlockSpec((rows, width), lambda i, dests: (0, dests[i]))
    return pl.pallas_call(
        cut_ffn_kernel,
        grid_spec=pltpu.PrefetchScalarGridSpec(
            num_scalar_prefetch=1,
            grid=(n,),
            in_specs=[block, block, pl.BlockSpec((rows, 1), lambda i, dests: (0, 0))],
            out_specs=pl.BlockSpec((1, rows, 2 * width), lambda i, dests: (i, 0, 0)),
        ),
        out_shape=jax.ShapeDtypeStruct((n, rows, 2 * width), BF),
    )(dests, w_gate, w_up, gain)


def term_kernel(count, m, spots, *refs):
    lefts, rights = refs[:count], refs[count : 2 * count]
    keep_ref, send_ref, held = refs[2 * count :]
    held[...] = sum(mm_t(z[...], g[...]) for z, g in zip(lefts, rights))
    rows = held.shape[0] // m
    core, side = spots[spots.shape[0] - 2], spots[spots.shape[0] - 1]
    for far in range(m // 2):
        for ref, choice in ((keep_ref, core), (send_ref, 1 - core)):
            owner = 2 * (side ^ far) + choice
            ref[far, 0] = held[pl.ds(pl.multiple_of(owner * rows, rows), rows), :].astype(BF)


def term(m, n, owners, f, lefts, rights):
    count = len(lefts)
    tokens, width = rights[0].shape
    block = lefts[0].shape[1] // n
    if n > 1 and block % 128:
        full = sum(mm_t(z, g) for z, g in zip(lefts, rights)).astype(BF)
        full = full.reshape(n, m // 2, 2, block // m, width)[owners].transpose(1, 2, 0, 3, 4)
        full = full[(f // 2) ^ jnp.arange(m // 2)]
        return pick(full, f % 2, 1), pick(full, 1 - f % 2, 1)
    out = pl.BlockSpec((m // 2, 1, block // m, width), lambda i, spots: (0, i, 0, 0))
    return pl.pallas_call(
        functools.partial(term_kernel, count, m),
        grid_spec=pltpu.PrefetchScalarGridSpec(
            num_scalar_prefetch=1,
            grid=(owners.shape[0],),
            in_specs=[pl.BlockSpec((tokens, block), lambda i, spots: (0, spots[i]))] * count
            + [pl.BlockSpec((tokens, width), lambda i, spots: (0, 0))] * count,
            out_specs=[out, out],
            scratch_shapes=[pltpu.VMEM((block, width), F32)],
        ),
        out_shape=[
            jax.ShapeDtypeStruct((m // 2, owners.shape[0], block // m, width), BF)
        ] * 2,
        compiler_params=pltpu.CompilerParams(vmem_limit_bytes=44 << 20),
        cost_estimate=pl.CostEstimate(
            flops=2 * count * tokens * owners.shape[0] * block * width,
            bytes_accessed=2 * owners.shape[0] * block * (count * tokens + width)
            + 2 * count * tokens * width,
            transcendentals=0,
        ),
    )(jnp.concatenate([owners, jnp.stack([f % 2, f // 2])]), *lefts, *rights)


def lanes(width):
    return lax.broadcasted_iota(jnp.int32, (1, width), 1)


def turned(x):
    half = HEAD_DIM // 2
    low = lanes(128) % HEAD_DIM < half
    return jnp.where(low, -pltpu.roll(x, 128 - half, 1), pltpu.roll(x, half, 1))


def in_halves(f, x):
    return jnp.concatenate([f(x[:, i : i + 128]) for i in range(0, x.shape[1], 128)], axis=1)


def fill_pads(heads, kv, row, kpad, vpad):
    width = kpad.shape[2]
    swapped = pltpu.roll(kv, HEAD_DIM, 1)
    first = lanes(128) < HEAD_DIM
    both_k = jnp.where(first, kv, swapped)
    both_v = jnp.where(first, swapped, kv)
    wide_k = jnp.concatenate([both_k] * (width // 128), axis=1)
    wide_v = jnp.concatenate([both_v] * (width // 128), axis=1)
    for h in range(heads):
        own = lanes(width) // HEAD_DIM == h
        kpad[h, row, :] = jnp.where(own, wide_k, 0.0).astype(BF)
        vpad[h, row, :] = jnp.where(own, wide_v, 0.0).astype(BF)


def key_rows(stream, each):
    step = 256

    @pl.loop(0, stream // step)
    def _(i):
        each(pl.ds(pl.multiple_of(i * step, step), step))


def hidden_bias(facts, table):
    seen = (facts[:, 64:65] == table[64:65, :]) & (table[65:66, :] <= facts[:, 65:66])
    return jnp.where(seen, 0.0, HIDE)


def spread_lanes(x):
    x = jnp.where(lanes(128) < 32, x, 0.0)
    x = x + pltpu.roll(x, 32, 1)
    return x + pltpu.roll(x, 64, 1)


def waves(facts):
    return spread_lanes(facts), spread_lanes(pltpu.roll(facts, 96, 1))


def attend_kernel(
    heads, base, act_ref, table_ref, facts_in, o_ref, lse_ref, q_ref, kv_ref, *rest
):
    kpad, vpad = rest[-2:]
    facts_ref = rest[0] if base == 0 else facts_in
    rows, width = q_ref.shape
    stream = act_ref.shape[0]

    @pl.when(pl.program_id(0) == 0)
    def _():
        def each(row):
            if base == 0:
                facts_ref[row, :] = table_ref[:, row].T
            cos, sin = waves(facts_ref[row, :])
            kv = act_ref[row, width : width + 128]
            rot = kv * cos + turned(kv) * sin
            kv = jnp.where(lanes(128) < HEAD_DIM, rot, kv)
            kv_ref[row, :] = kv.astype(BF)
            fill_pads(heads, kv, row, kpad, vpad)

        key_rows(stream, each)

    here = pl.ds(pl.multiple_of(base + pl.program_id(0) * rows, rows), rows)
    facts = facts_ref[here, :]
    cos, sin = waves(facts)
    q = in_halves(lambda x: x * cos + turned(x) * sin, act_ref[here, :width])
    q = (q * (1.0 / math.sqrt(HEAD_DIM))).astype(BF)
    q_ref[...] = q
    bias = hidden_bias(facts, table_ref)
    out = jnp.zeros((rows, width), F32)
    lse = jnp.zeros((rows, 128), F32)
    for h in range(heads):
        s = against(q, kpad[h]) + bias
        top = jnp.max(s, axis=1, keepdims=True)
        p = jnp.exp(s - top)
        total = jnp.sum(p, axis=1, keepdims=True)
        out = out + mm(p.astype(BF), vpad[h]) / total
        lse = jnp.where(lanes(128) == h, top + jnp.log(total), lse)
    o_ref[...] = out.astype(BF)
    lse_ref[...] = lse


def attend_back_kernel(
    heads, base, first, q_ref, g_ref, kv_ref, table_ref, facts_ref, inv_ref, lse_ref, *rest
):
    if first:
        ga_ref, gs_ref, dk_out, dv_out, kpad, vpad, dk, dv = rest
    else:
        dk_in, dv_in, ga_ref, gs_ref, kv_ga, kv_gs, kpad, vpad, dk, dv = rest
    rows, width = q_ref.shape
    stream = kv_ref.shape[0]

    @pl.when(pl.program_id(0) == 0)
    def _():
        key_rows(stream, lambda row: fill_pads(heads, kv_ref[row, :].astype(F32), row, kpad, vpad))
        dk[...] = jnp.zeros_like(dk) if first else dk_in[...]
        dv[...] = jnp.zeros_like(dv) if first else dv_in[...]

    here = pl.ds(pl.multiple_of(base + pl.program_id(0) * rows, rows), rows)
    bias = hidden_bias(facts_ref[here, :], table_ref)
    q = q_ref[...]
    g = g_ref[...]
    dq = jnp.zeros((rows, width), F32)
    for h in range(heads):
        p = jnp.exp(against(q, kpad[h]) + (bias - lse_ref[:, h : h + 1]))
        dp = against(g, vpad[h])
        delta = jnp.sum(p * dp, axis=1, keepdims=True)
        ds = (p * (dp - delta)).astype(BF)
        dq = dq + mm(ds, kpad[h])
        own = lanes(width) // HEAD_DIM == h
        dk[...] += mm_t(ds, jnp.where(own, q, 0).astype(BF))
        dv[...] += mm_t(p.astype(BF), jnp.where(own, g, 0).astype(BF))
    dq = dq * (1.0 / math.sqrt(HEAD_DIM))

    def turn_back(row, x):
        cos, sin = waves(facts_ref[row, :])
        return x * cos - turned(x * sin)

    ga = in_halves(lambda x: turn_back(here, x), dq)
    ga_ref[...] = ga.astype(BF)
    gs_ref[...] = (ga * inv_ref[here, :]).astype(BF)

    @pl.when(pl.program_id(0) == pl.num_programs(0) - 1)
    def _():
        if first:
            dk_out[...] = dk[...]
            dv_out[...] = dv[...]
            return

        def folded(x):
            x = sum(x[:, i : i + 128] for i in range(0, width, 128))
            return x + pltpu.roll(x, HEAD_DIM, 1)

        def each(row):
            gk = turn_back(row, folded(dk[row, :]))
            gkv = jnp.where(lanes(128) < HEAD_DIM, gk, folded(dv[row, :]))
            kv_ga[row, :] = gkv.astype(BF)
            kv_gs[row, :] = (gkv * inv_ref[row, :]).astype(BF)

        key_rows(stream, each)


def attend_specs(rows, stream, base):
    def part(width):
        return pl.BlockSpec((rows, width), lambda i: (i, 0))

    def by_row(width):
        return pl.BlockSpec((rows, width), lambda i: (i + base // rows, 0))

    def whole(width):
        return pl.BlockSpec((stream, width), lambda i: (0, 0))

    return part, by_row, whole


def attend(heads, half, act, table, facts=None):
    stream, width = act.shape
    width, count = width - 128, stream // 2
    base = half * count
    rows = 256 if stream <= 1024 else 128
    part, by_row, whole = attend_specs(rows, stream, base)
    first = half == 0
    return pl.pallas_call(
        functools.partial(attend_kernel, heads, base),
        grid=(count // rows,),
        in_specs=[
            whole(width + 128),
            pl.BlockSpec((128, stream), lambda i: (0, 0)),
            pl.BlockSpec((8, 128), lambda i: (0, 0)) if first else whole(128),
        ],
        out_specs=[part(width), part(128), part(width), whole(128)] + [whole(128)] * first,
        out_shape=[
            jax.ShapeDtypeStruct((count, width), BF),
            jax.ShapeDtypeStruct((count, 128), F32),
            jax.ShapeDtypeStruct((count, width), BF),
            jax.ShapeDtypeStruct((stream, 128), BF),
        ]
        + [jax.ShapeDtypeStruct((stream, 128), F32)] * first,
        scratch_shapes=[pltpu.VMEM((heads, stream, width), BF)] * 2,
        compiler_params=pltpu.CompilerParams(vmem_limit_bytes=44 << 20),
        cost_estimate=pl.CostEstimate(
            flops=4 * stream * count * heads * 256,
            bytes_accessed=8 * stream * width,
            transcendentals=stream * count * heads,
        ),
    )(act, table, jnp.zeros((8, 128), F32) if first else facts)


def attend_back(heads, half, q, g, kv, table, facts, inverse, lse, sums=()):
    count, width = q.shape
    stream = kv.shape[0]
    base = half * count
    rows = 256 if stream <= 1024 else 128
    part, by_row, whole = attend_specs(rows, stream, base)
    first = half == 0
    last_width, last_type = (width, F32) if first else (128, BF)
    return pl.pallas_call(
        functools.partial(attend_back_kernel, heads, base, first),
        grid=(count // rows,),
        in_specs=[
            part(width), part(width), whole(128),
            pl.BlockSpec((128, stream), lambda i: (0, 0)), whole(128), whole(1), part(128),
        ] + [whole(width)] * len(sums),
        out_specs=[part(width)] * 2 + [whole(last_width)] * 2,
        out_shape=[jax.ShapeDtypeStruct((count, width), BF)] * 2
        + [jax.ShapeDtypeStruct((stream, last_width), last_type)] * 2,
        scratch_shapes=[
            *([pltpu.VMEM((heads, stream, width), BF)] * 2),
            *([pltpu.VMEM((stream, width), F32)] * 2),
        ],
        compiler_params=pltpu.CompilerParams(vmem_limit_bytes=48 << 20),
        cost_estimate=pl.CostEstimate(
            flops=10 * stream * count * heads * 256,
            bytes_accessed=20 * stream * width,
            transcendentals=stream * count * heads,
        ),
    )(q, g, kv, table, facts, inverse, lse, *sums)


def finish_ffn_kernel(n, spots, *refs):
    gate_ref, up_ref, gain_ref, og_ref, ou_ref, gg_ref = refs[n:]
    width = gate_ref.shape[1]
    gain = gain_ref[...]
    step = pl.program_id(0)

    @pl.when(step == 0)
    def _():
        gg_ref[...] = jnp.zeros_like(gg_ref)

    for k in range(n):

        @pl.when(step == k)
        def _(piece=refs[k]):
            gate = piece[:, :width].astype(F32)
            up = piece[:, width:].astype(F32)
            og_ref[...] = gate * gain
            ou_ref[...] = up * gain
            term = jnp.sum(
                gate * gate_ref[...].astype(F32) + up * up_ref[...].astype(F32),
                axis=1,
                keepdims=True,
            )
            gg_ref[...] += jnp.broadcast_to(term, gg_ref.shape)


def finish_ffn(pieces, spots, w_gate, w_up, gain):
    n = len(pieces)
    rows, both = pieces[0].shape
    width = both // 2
    block = pl.BlockSpec((rows, width), lambda i, spots: (0, spots[i]))
    return pl.pallas_call(
        functools.partial(finish_ffn_kernel, n),
        grid_spec=pltpu.PrefetchScalarGridSpec(
            num_scalar_prefetch=1,
            grid=(n,),
            in_specs=[pl.BlockSpec((rows, both), lambda i, spots: (0, 0))] * n
            + [block, block, pl.BlockSpec((rows, 1), lambda i, spots: (0, 0))],
            out_specs=[block, block, pl.BlockSpec((rows, 128), lambda i, spots: (0, 0))],
        ),
        out_shape=[
            jax.ShapeDtypeStruct(w_gate.shape, F32),
            jax.ShapeDtypeStruct(w_gate.shape, F32),
            jax.ShapeDtypeStruct((rows, 128), F32),
        ],
        compiler_params=pltpu.CompilerParams(vmem_limit_bytes=24 << 20),
    )(spots, *pieces, w_gate, w_up, gain)


def finish_qkv_kernel(n, spots, pieces, q_ref, k_ref, v_ref, gain_ref, oq, ok, ov, gg_ref):
    q_width = q_ref.shape[1] // n
    sharers = n // KV_HEADS
    gain = gain_ref[...]
    term = jnp.zeros((q_ref.shape[0], 1), F32)
    for kv in range(KV_HEADS):
        held = 0.0
        for j in range(sharers):
            c = kv * sharers + j
            piece = pieces[spots[c]].astype(F32)
            here = slice(c * q_width, (c + 1) * q_width)
            q = piece[:, :q_width]
            held = held + piece[:, q_width:]
            oq[:, here] = q * gain
            term += jnp.sum(q * q_ref[:, here].astype(F32), axis=1, keepdims=True)
        here = slice(kv * HEAD_DIM, (kv + 1) * HEAD_DIM)
        k, v = held[:, :HEAD_DIM], held[:, HEAD_DIM:]
        ok[:, here] = k * gain
        ov[:, here] = v * gain
        term += jnp.sum(
            k * k_ref[:, here].astype(F32) + v * v_ref[:, here].astype(F32), axis=1, keepdims=True
        )
    gg_ref[...] = jnp.broadcast_to(term, gg_ref.shape)


def finish_qkv(pieces, spots, w_query, w_key, w_value, gain):
    n, rows, _ = pieces.shape
    vmem = pl.BlockSpec(memory_space=pltpu.VMEM)
    return pl.pallas_call(
        functools.partial(finish_qkv_kernel, n),
        in_specs=[pl.BlockSpec(memory_space=pltpu.SMEM)] + [vmem] * 5,
        out_specs=[vmem] * 4,
        out_shape=[
            jax.ShapeDtypeStruct(w_query.shape, F32),
            jax.ShapeDtypeStruct(w_key.shape, F32),
            jax.ShapeDtypeStruct(w_value.shape, F32),
            jax.ShapeDtypeStruct((rows, 128), F32),
        ],
    )(spots, pieces, w_query, w_key, w_value, gain)


def norm_back(grad_scaled, unit_rows, inverse):
    return inverse * (
        grad_scaled - unit_rows * jnp.mean(grad_scaled * unit_rows, axis=1, keepdims=True)
    )


def rms_inverse(values):
    return lax.rsqrt(jnp.mean(values * values, axis=1, keepdims=True) + EPSILON)


def body(
    tokens,
    teacher,
    valid_mask,
    lengths,
    span_order,
    w_query,
    w_key,
    w_value,
    w_out,
    w_gate,
    w_up,
    w_down,
    gain_attn,
    gain_ffn,
):
    net = Links()
    n, m, ring = net.n, net.m, net.ring
    x_low = tokens[0]
    tok_rows, width = x_low.shape
    rows = w_query.shape[0]
    heads = HEADS // n
    q_width = heads * HEAD_DIM
    sharers = n // KV_HEADS
    ff_slice = w_gate.shape[1] // n
    stream = tok_rows * n
    spans = tok_rows // SPAN

    jobs, box = net.jobs, net.box

    def later(name, key, job):
        jobs.setdefault(name, {})[key] = job

    def core(x):
        return net.flip(x, "fsdp", 1)

    def side(x):
        return net.flip(x, "fsdp", 2)

    gain_a = gain_attn.astype(F32)[:, None]
    gain_f = gain_ffn.astype(F32)[:, None]
    routes, origins = net.routes(), net.origins()
    pair_moves = [(da, dq) for da in range(ring) for dq in range(2)]
    dests, sources = net.dests(pair_moves), net.sources(pair_moves)
    span_row = jnp.broadcast_to(
        jnp.pad(span_order[0].astype(BF), (0, q_width + 2 * HEAD_DIM - spans))[None, :],
        (16, q_width + 2 * HEAD_DIM),
    )
    straight, across = cut_qkv(n, routes, w_query, w_key, w_value, gain_a, span_row)

    def along(first, other):
        def job(begun):
            ready = tie(jnp.stack([first, box[other]], axis=1), begun)
            return [net.shift(ready[da], da, 0) if da else ready[da] for da in range(ring)]

        return job

    half_rows = w_down.shape[0] // 2
    later("ax0", "q_across", lambda begun: net.shift(across, 0, 1))
    later("ax1", "out_side", lambda begun: side(tie(w_out, begun)))
    later("ax0", "down_side_0", lambda begun: side(w_down[:half_rows]))
    later("ax1", "q_came", along(straight, "q_across"))

    def q_side(begun):
        came = jnp.concatenate(box["q_came"], axis=0)
        return came, side(came)

    later("ax2", "q_sides", q_side)
    later("ax2", "out_core", lambda begun: [core(tie(w_out, begun)), core(box["out_side"])])
    later("ax3", "down_side_1", lambda begun: side(tie(w_down[half_rows:], begun)))
    token_blocks = net.gather_ctx(x_low, "ax")
    q_came, q_other = box["q_sides"]
    qkv_w = net.assemble([[q_came, core(q_came), q_other, core(q_other)]], sources, rows)
    spans_here = tie(q_came, qkv_w)[:, rows, :spans].astype(jnp.int32).reshape(n * spans)
    padding = (-q_width) % 128

    def with_padding(array):
        if not padding:
            return array
        return jnp.concatenate(
            [
                jnp.pad(array[:, :q_width], ((0, 0), (0, padding))),
                array[:, q_width:],
            ],
            axis=1,
        )

    def no_padding(array):
        if not padding:
            return array
        return jnp.concatenate([array[:, :q_width], array[:, q_width + padding :]], axis=1)

    qkv_w = with_padding(qkv_w)
    alone = jnp.zeros((1,), jnp.int32)
    out_w = net.assemble(
        [[x[None] for x in (w_out, box["out_core"][0], box["out_side"], box["out_core"][1])]],
        alone,
        rows,
    )

    direct = net.direct()
    quarter = n // 4
    gate_in, up_in = tie((w_gate, w_up), token_blocks[1][0][0])
    gate_up_cut = cut_ffn(net.dests(direct), gate_in, up_in, gain_f)
    came_ffn = [gate_up_cut[0]]

    def send(pieces, begun, start, stop):
        pieces = tie(pieces, begun)
        return [net.shift(pieces[i], *direct[i]) for i in range(start, stop)]

    place = (
        spans_here[:, None] * SPAN + lax.broadcasted_iota(jnp.int32, (n * spans, SPAN), 1)
    ).reshape(stream)
    seq_ends = jnp.cumsum(lengths[0])
    passed = seq_ends[None, :] <= place[:, None]
    segment = jnp.sum(passed.astype(jnp.int32), axis=1)
    seq_begin = jnp.sum(jnp.where(passed, lengths[0][None, :], 0), axis=1)
    rates = jnp.asarray(rope_rates(HEAD_DIM)[: HEAD_DIM // 2])
    angles = rates[:, None] * (place - seq_begin).astype(F32)[None, :]
    table = jnp.concatenate(
        [
            jnp.cos(angles),
            jnp.sin(angles),
            segment.astype(F32)[None, :],
            place.astype(F32)[None, :],
            jnp.zeros((128 - 66, stream), F32),
        ],
        axis=0,
    )

    x_pairs, inverses, acts_attn = [], [], []
    pair_rows = 2 * tok_rows
    for r in range(ring):
        x_pair = paired(token_blocks[r])
        inverse = rms_inverse(x_pair.astype(F32))
        x_pairs.append(x_pair)
        inverses.append(inverse)
        acts_attn.append(mm(x_pair, qkv_w) * inverse)
    inverse_all = jnp.concatenate(inverses, axis=0)
    act_all = jnp.concatenate(acts_attn, axis=0)
    cuts = [1, max(1, 0 * n // 8), 4 * n // 8, 6 * n // 8, 7 * n // 8, n]
    first = attend(heads, 0, act_all, table)
    sent = send(gate_up_cut, qkv_w, cuts[1], cuts[2])
    act_all, sent = lax.optimization_barrier((act_all, sent))
    came_ffn += sent
    facts = first[4]
    second = attend(heads, 1, act_all, table, facts)
    kv_rot = second[3]
    attended_halves = first[0], second[0]

    def split_pair(block):
        return block[:tok_rows], block[tok_rows:]

    def pair_of(array, r):
        return array[r * pair_rows : (r + 1) * pair_rows]

    inputs = x_low.astype(F32)

    def of_halves(halves, r):
        which, start = divmod(r * pair_rows, stream // 2)
        return halves[which][start : start + pair_rows]

    for i in range(3):
        later(f"ro{i}", f"f_{i}", lambda begun, i=i: send(gate_up_cut, begun, cuts[2 + i], cuts[3 + i]))
    for g in range(4):

        def g_side(begun, g=g):
            pieces = came_ffn + sum((box[f"f_{i}"] for i in range(g)), [])
            block = tie(jnp.stack(pieces[g * quarter : (g + 1) * quarter]), begun)
            return block, side(block)

        def g_core(begun, g=g):
            return [core(x) for x in box[f"g_side{g}"]]

        later(f"ro{g}", f"g_side{g}", g_side)
        later(f"ro{g + 1}" if g < 3 else "ff0", f"g_core{g}", g_core)
    later("ro0", "down_core", lambda begun: core(tie(w_down, begun)))

    def down_far(begun):
        return core(jnp.concatenate([box["down_side_0"], box["down_side_1"]], axis=0))

    later("ff0", "down_far", down_far)
    middle = inputs + net.scatter_ctx(
        lambda r: split_pair(mm(of_halves(attended_halves, r)[:, :q_width], out_w)), "ro"
    )

    inverse_ffn = rms_inverse(middle)
    unit_ffn = middle * inverse_ffn
    unit_blocks = net.gather_ctx(unit_ffn.astype(BF), "ff")
    gate_up_w = net.assemble(
        [
            [box[f"g_side{g}"][0], box[f"g_core{g}"][0], box[f"g_side{g}"][1], box[f"g_core{g}"][1]]
            for g in range(4)
        ],
        net.sources(direct),
        rows,
    )
    down_sides = jnp.concatenate([box["down_side_0"], box["down_side_1"]], axis=0)
    down_w = net.assemble(
        [[x[None] for x in (w_down, box["down_core"], down_sides, box["down_far"])]],
        alone,
        w_down.shape[0],
    )
    z_pairs = [paired(blocks) for blocks in unit_blocks]
    acts, hiddens = {}, {}

    def down_part(r):
        both = mm(z_pairs[r], gate_up_w)
        gate, up = both[:, :ff_slice], both[:, ff_slice:]
        acts[r] = (gate, up)
        hiddens[r] = (gate * jax.nn.sigmoid(gate) * up).astype(BF)
        return split_pair(mm(hiddens[r], down_w))

    out_full = middle + net.scatter_ctx(down_part, "fo")

    valid_f = valid_mask[0].astype(F32)[:, None]
    missed = (out_full - teacher[0].astype(F32)) * valid_f
    sums = jnp.stack([jnp.sum(missed * missed), jnp.sum(valid_f)]).reshape(1, 2)
    grad_out = missed

    grad_blocks = net.gather_ctx(grad_out.astype(BF), "bf")
    grad_pairs = [paired(blocks) for blocks in grad_blocks]
    grad_acts = {}

    def unit_part(r):
        gate, up = acts[r]
        grad_hidden = against(grad_pairs[r], down_w)
        share = jax.nn.sigmoid(gate)
        grad_gate = grad_hidden * up * share * (1.0 + gate * (1.0 - share))
        grad_up = grad_hidden * (gate * share)
        grad_acts[r] = jnp.concatenate([grad_gate.astype(BF), grad_up.astype(BF)], axis=1)
        return split_pair(against(grad_acts[r], gate_up_w))

    owners = net.dests(direct)
    term_slots = ["bo2", "bo3", "am0", "am1", "am2", "am3", "ar0"]

    def listed(items):
        return [items[r] for r in range(ring)]

    for g in range(4):

        def g_term(begun, g=g):
            lefts, rights = tie((z_pairs, listed(grad_acts)), begun)
            return term(m, n, owners[g * quarter : (g + 1) * quarter], net.f, lefts, rights)

        def g_cross(begun, g=g):
            return core(box[f"t{g}"][1])

        def g_far(begun, g=g):
            keep, got = box[f"t{g}"][0], box[f"tc{g}"]
            return side((keep[1].astype(F32) + got[1]).astype(BF))

        later(term_slots[g], f"t{g}", g_term)
        later(term_slots[g + 1], f"tc{g}", g_cross)
        later(term_slots[g + 2], f"ts{g}", g_far)

    def d_term(begun):
        lefts, rights = tie((listed(hiddens), grad_pairs), begun)
        return term(m, 1, alone, net.f, lefts, rights)

    later("am2", "d", d_term)
    later("am3", "dc", lambda begun: core(box["d"][1]))

    def d_far(begun):
        block = (tie(box["d"][0], begun)[1, 0].astype(F32) + box["dc"][1, 0]).astype(BF)
        return block[half_rows:], side(block[:half_rows])


    axes = [("ctx", 1 << i) for i in range((n - 1).bit_length())]
    axes += [("fsdp", 1 << i) for i in range((m - 1).bit_length())]
    spots = [f"am{r}" for r in range(ring)] + [f"ar{r}" for r in range(ring)]
    box["sums"] = sums
    for name, (axis, bit) in zip(spots, axes):
        later(name, "sums", lambda begun, a=axis, b=bit: box["sums"] + net.flip(tie(box["sums"], begun), a, b))

    unit_parts = {r: unit_part(r) for r in net.scatter_order()}
    grad_unit = net.scatter_ctx(unit_parts.get, "bo")
    grad_middle = grad_out + norm_back(grad_unit, unit_ffn, inverse_ffn)
    middle_low = grad_middle.astype(BF)

    middle_blocks = net.gather_ctx(middle_low, "am")
    middle_pairs = [paired(blocks) for blocks in middle_blocks]

    def summed(i):
        g, at = divmod(i, quarter)
        keep, got, far = box[f"t{g}"][0], box[f"tc{g}"], box[f"ts{g}"]
        return (keep[0, at].astype(F32) + got[0, at] + far[at]).astype(BF)

    def send_sum(begun, start, stop):
        return [net.shift(tie(summed(i), begun), *direct[i]) for i in range(start, stop)]

    def back_half(half):
        parts = [
            against(middle_pairs[r], out_w).astype(BF)
            for r in range(half * ring // 2, (half + 1) * ring // 2)
        ]
        grads = jnp.concatenate(parts, axis=0)
        return jnp.pad(grads, ((0, 0), (0, padding))) if padding else grads

    grads_first, grads_second = back_half(0), back_half(1)
    came_sums = [summed(0)]
    cuts = [1, 3 * n // 8, 5 * n // 8, 7 * n // 8, n]
    sent = send_sum(middle_blocks[-1][0][0], cuts[0], cuts[1])
    grads_first, grads_second, sent = lax.optimization_barrier((grads_first, grads_second, sent))
    came_sums += sent
    fixed = kv_rot, table, facts, inverse_all
    sent, box["ds0"] = send_sum(grads_first, cuts[1], cuts[2]), d_far(grads_first)
    backed = attend_back(heads, 0, first[2], grads_first, *fixed, first[1])
    backed, grads_second, sent, box["ds0"] = lax.optimization_barrier(
        (backed, grads_second, sent, box["ds0"])
    )
    came_sums += sent
    gq_first, gs_first, sum_k, sum_v = backed
    sent = send_sum(grads_second, cuts[2], cuts[3])
    box["ds1"] = side(tie(box["ds0"][0], grads_second))
    backed = attend_back(heads, 1, second[2], grads_second, *fixed, second[1], (sum_k, sum_v))
    (gq_second, gs_second, g_kv, gs_kv), sent, box["ds1"] = lax.optimization_barrier(
        (backed, sent, box["ds1"])
    )
    came_sums += sent

    def attn_part(r):
        rows_q = of_halves((gq_first, gq_second), r)
        grads = jnp.concatenate([rows_q, pair_of(g_kv, r)], axis=1)
        return split_pair(against(grads, qkv_w))

    def q_term(begun):
        grads = [
            jnp.concatenate([of_halves((gs_first, gs_second), r), pair_of(gs_kv, r)], axis=1)
            for r in range(ring)
        ]
        lefts, grads = tie((x_pairs, grads), begun)
        return term(m, n, dests, net.f, lefts, grads)

    def q_back(begun):
        (keep, _), got = box["qt"], box["qc"]
        block = keep[0].astype(F32) + got[0] + box["qs"]
        if padding:
            block = jnp.concatenate([block[..., :q_width], block[..., q_width + padding :]], axis=2)
        block = block.astype(BF).reshape(ring, 2, rows, q_width + 2 * HEAD_DIM)
        return block[:, 0], net.shift(block[:, 1], 0, 1)

    def q_along(begun):
        ready = tie(jnp.stack(box["qb"], axis=1), begun)
        return [net.shift(ready[da], da, 0) if da else ready[da] for da in range(ring)]

    def o_term(begun):
        lefts = [of_halves(attended_halves, r)[:, :q_width] for r in range(ring)]
        lefts, grads = tie((lefts, middle_pairs), begun)
        return term(m, 1, alone, net.f, lefts, grads)

    def crossed(key, made):
        return lambda begun: core(tie(box[made][1], begun))

    def farther(made, got):
        return lambda begun: side((box[made][0][1].astype(F32) + box[got][1]).astype(BF))

    def ends(begun):
        square_sum, valid_count = box["sums"][0, 0], box["sums"][0, 1]
        box["loss"] = 0.5 * square_sum / (width * valid_count)
        box["spread"] = (tok_rows * n * m) / valid_count
        pieces = tie(came_sums + box["c_last"], begun)
        return finish_ffn(pieces, net.sources(direct), w_gate, w_up, gain_f * box["spread"])

    later("ar0", "ot", o_term)
    later("ar0", "qt", q_term)
    later("ar0", "c_last", lambda begun: send_sum(begun, cuts[3], n))
    later("ar1", "qc", crossed("qc", "qt"))
    later("ar1", "oc", crossed("oc", "ot"))
    later("ar2", "qs", farther("qt", "qc"))
    later("ar2", "os", farther("ot", "oc"))
    later("ar3", "qb", q_back)
    later(f"ar{max(2, len(axes) - ring)}", "ffn", ends)
    grad_attn = net.scatter_ctx(attn_part, "ar")
    spread = box["spread"]
    inverse_attn = rms_inverse(inputs)
    grad_input = grad_middle + norm_back(grad_attn, inputs * inverse_attn, inverse_attn)
    grad_w_query, grad_w_key, grad_w_value, gain_sum_attn = finish_qkv(
        jnp.concatenate(q_along(grad_attn), axis=0), origins, w_query, w_key, w_value, gain_a * spread
    )
    grad_w_out = (box["ot"][0][0, 0].astype(F32) + box["oc"][0, 0] + box["os"][0]) * spread
    down_keep = box["d"][0][0, 0].astype(F32) + box["dc"][0, 0]
    down_far = jnp.concatenate([box["ds0"][1], box["ds1"]], axis=0)
    grad_down = down_keep + down_far
    grad_w_gate, grad_w_up, gain_sum_ffn = box["ffn"]
    loss_value = box["loss"]
    return (
        out_full.astype(BF)[None],
        loss_value,
        (grad_input * spread)[None],
        grad_w_query,
        grad_w_key,
        grad_w_value,
        grad_w_out,
        grad_w_gate,
        grad_w_up,
        grad_down * spread,
        gain_sum_attn[:, 0] * spread,
        gain_sum_ffn[:, 0] * spread,
    )


def solution(mesh):
    token_spec = P("fsdp", "ctx", None)
    row_spec = P(("ctx", "fsdp"), None)
    gain_spec = P(("ctx", "fsdp"))
    in_specs = (
        token_spec,
        token_spec,
        P("fsdp", "ctx"),
        P("fsdp", None),
        P("fsdp", "ctx"),
        *([row_spec] * 7),
        gain_spec,
        gain_spec,
    )
    out_specs = (token_spec, P(), token_spec, *([row_spec] * 7), gain_spec, gain_spec)
    return jax.shard_map(body, mesh=mesh, in_specs=in_specs, out_specs=out_specs, check_vma=False)
```

```python
import functools
import math

import jax
import jax.numpy as jnp
import numpy as np
from jax import lax
from jax.experimental import pallas as pl
from jax.experimental.pallas import tpu as pltpu
from jax.sharding import PartitionSpec as P

HEADS = 32
KV_HEADS = 8
HEAD_DIM = 64
SPAN = 128
EPSILON = 1e-05
HIDE = -1e30
TWICE = ("bf", "bo")
BF = jnp.bfloat16
F32 = jnp.float32


def rope_rates(head_width):
    frequency = 1.0 / 500000.0 ** (np.arange(0, head_width, 2) / head_width)
    wavelength = 2.0 * np.pi / frequency
    blend_share = (8192.0 / wavelength - 1.0) / 3.0
    blended = (1.0 - blend_share) * frequency / 32.0 + blend_share * frequency
    frequency = np.where(
        wavelength < 2048.0, frequency, np.where(wavelength > 8192.0, frequency / 32.0, blended)
    )
    return np.concatenate([frequency, frequency]).astype(np.float32)


def mm(left, right):
    return jnp.dot(left, right, preferred_element_type=F32)


def mm_t(left, right):
    return lax.dot_general(left, right, (((0,), (0,)), ((), ())), preferred_element_type=F32)


def against(left, right):
    return lax.dot_general(left, right, (((1,), (1,)), ((), ())), preferred_element_type=F32)


def pick(array, index, axis=0):
    return lax.dynamic_index_in_dim(array, index, axis, keepdims=False)


def paired(blocks):
    rows = [jnp.concatenate(pieces, axis=1) if len(pieces) > 1 else pieces[0] for pieces in blocks]
    return jnp.concatenate(rows, axis=0)


def tie(value, *others):
    return lax.optimization_barrier((value, *others))[0]


class Links:
    def __init__(self):
        self.n = lax.axis_size("ctx")
        self.m = lax.axis_size("fsdp")
        self.ring = self.n // 2
        self.c = lax.axis_index("ctx")
        self.f = lax.axis_index("fsdp")
        self.a = self.c // 2
        self.b = self.c % 2
        self.box, self.jobs = {}, {}

    def shift(self, x, da, dq):
        perm = [
            (a * 2 + b, ((a + da) % self.ring) * 2 + (b ^ dq))
            for a in range(self.ring)
            for b in range(2)
        ]
        return lax.ppermute(x, "ctx", perm)

    def flip(self, x, axis, bit):
        size = self.n if axis == "ctx" else self.m
        return lax.ppermute(x, axis, [(i, i ^ bit) for i in range(size)])

    def slot(self, name, begun, mains):
        made = {key: job(begun) for key, job in self.jobs.pop(name, {}).items()}
        mains, made = lax.optimization_barrier((mains, made))
        self.box.update(made)
        return mains

    def cut(self, x, name):
        count = 2 if name in TWICE else 1
        step = x.shape[1] // count
        return [x[:, i * step : (i + 1) * step] for i in range(count)]

    def gather_ctx(self, x, name):
        out = []
        held = self.cut(x, name)
        for r in range(self.ring):
            pairs, moved = [], []
            for i, piece in enumerate(held):
                mains = [self.shift(piece, 0, 1)]
                if r < self.ring - 1:
                    mains.append(self.shift(piece, 1, 0))
                last = i == len(held) - 1
                mains = self.slot(f"{name}{r}" if last else "", piece, mains)
                pairs.append(mains[0])
                moved.append(mains[-1])
            out.append((held, pairs))
            held = moved
        return out

    def scatter_order(self):
        return list(range(1, self.ring)) + [0]

    def scatter_ctx(self, part, name):
        count = len(self.cut(jnp.zeros((1, 2)), name))
        held, got = [None] * count, [None] * count
        for i, r in enumerate(self.scatter_order()):
            mine, other = part(r)
            pieces = zip(self.cut(mine, name), self.cut(other.astype(BF), name))
            for k, (own, away) in enumerate(pieces):
                if i:
                    away = tie(away, got[k])
                mains = [self.shift(away, 0, 1)]
                if i:
                    mains.append(self.shift(held[k].astype(BF), 1, 0))
                mains = self.slot(f"{name}{i}" if k == count - 1 else "", away, mains)
                got[k] = mains[0]
                held[k] = own + sum(block.astype(F32) for block in mains)
        return held[0] if count == 1 else jnp.concatenate(held, axis=1)

    def direct(self):
        near = sorted(range(1, self.ring), key=lambda da: (min(da, self.ring - da), da))
        return [(0, 0)] + [(da, 0) for da in near] + [(0, 1)] + [(da, 1) for da in near]

    def dests(self, moves):
        spots = [((self.a + da) % self.ring) * 2 + (self.b ^ dq) for da, dq in moves]
        return jnp.stack(spots).astype(jnp.int32)

    def sources(self, moves):
        return self.dests([((self.ring - da) % self.ring, dq) for da, dq in moves])

    def routes(self):
        c = jnp.arange(self.n, dtype=jnp.int32)
        return ((c // 2 + self.ring - self.a) % self.ring) * 2 + (self.b ^ (c % 2))

    def origins(self):
        c = jnp.arange(self.n, dtype=jnp.int32)
        return ((self.a + self.ring - c // 2) % self.ring) * 2 + (self.b ^ (c % 2))

    def assemble(self, groups, spots, rows):
        sizes = [group[0].shape[0] for group in groups]
        count = sum(sizes)
        held_rows, width = groups[0][0].shape[1:]
        parts = max(1, min(width // 256, 8 // count))
        part = width // parts
        marks = self.f ^ jnp.arange(self.m, dtype=jnp.int32)
        specs, base = [], 0
        for size in sizes:

            def at(i, j, spots, base=base, size=size):
                return jnp.clip(i - base, 0, size - 1), 0, j

            specs += [pl.BlockSpec((1, held_rows, part), at)] * self.m
            base += size
        out = pl.pallas_call(
            functools.partial(place_kernel, sizes, self.m),
            grid_spec=pltpu.PrefetchScalarGridSpec(
                num_scalar_prefetch=1,
                grid=(count, parts),
                in_specs=specs,
                out_specs=pl.BlockSpec(
                    (1, self.m, rows, part), lambda i, j, spots: (spots[i], 0, 0, j)
                ),
            ),
            out_shape=jax.ShapeDtypeStruct((count, self.m, rows, width), BF),
            compiler_params=pltpu.CompilerParams(vmem_limit_bytes=24 << 20),
            cost_estimate=pl.CostEstimate(
                flops=0, bytes_accessed=4 * count * self.m * rows * width, transcendentals=0
            ),
        )(jnp.concatenate([spots, marks]), *[block for group in groups for block in group])
        return out.reshape(count * self.m * rows, width)


def place_kernel(sizes, m, spots, *refs):
    count = sum(sizes)
    out = refs[-1]
    base = 0
    for g, size in enumerate(sizes):

        @pl.when((pl.program_id(0) >= base) & (pl.program_id(0) < base + size))
        def _(g=g):
            for k in range(m):
                out[0, spots[count + k]] = refs[g * m + k][0, : out.shape[2]]

        base += size


def cut_qkv_kernel(n, spots, q_ref, k_ref, v_ref, gain_ref, span_ref, straight, across):
    rows = q_ref.shape[0]
    q_width = q_ref.shape[1] // n
    sharers = n // KV_HEADS
    gain = gain_ref[...]

    def folded(ref, i, width):
        return (ref[:, i * width : (i + 1) * width].astype(F32) * gain).astype(BF)

    for c in range(n):
        kv = c // sharers
        piece = jnp.concatenate(
            [
                folded(q_ref, c, q_width),
                folded(k_ref, kv, HEAD_DIM),
                folded(v_ref, kv, HEAD_DIM),
            ],
            axis=1,
        )
        move = spots[c]

        def fill(ref, piece=piece, move=move):
            ref[move // 2, :rows, :] = piece
            ref[move // 2, rows:, :] = jnp.broadcast_to(
                span_ref[0:16, : piece.shape[1]], (16, piece.shape[1])
            )

        pl.when(move % 2 == 0)(functools.partial(fill, straight))
        pl.when(move % 2 == 1)(functools.partial(fill, across))


def cut_qkv(n, spots, w_query, w_key, w_value, gain, span):
    rows = w_query.shape[0]
    width = w_query.shape[1] // n + 2 * HEAD_DIM
    vmem = pl.BlockSpec(memory_space=pltpu.VMEM)
    return pl.pallas_call(
        functools.partial(cut_qkv_kernel, n),
        in_specs=[pl.BlockSpec(memory_space=pltpu.SMEM)] + [vmem] * 5,
        out_specs=[vmem] * 2,
        out_shape=[jax.ShapeDtypeStruct((n // 2, rows + 16, width), BF)] * 2,
    )(spots, w_query, w_key, w_value, gain, span)


def cut_ffn_kernel(spots, gate, up, gain_ref, out):
    gain = gain_ref[...]
    width = gate.shape[1]
    out[0, :, :width] = (gate[...].astype(F32) * gain).astype(BF)
    out[0, :, width:] = (up[...].astype(F32) * gain).astype(BF)


def cut_ffn(dests, w_gate, w_up, gain):
    n = dests.shape[0]
    rows, width = w_gate.shape[0], w_gate.shape[1] // n
    block = pl.BlockSpec((rows, width), lambda i, dests: (0, dests[i]))
    return pl.pallas_call(
        cut_ffn_kernel,
        grid_spec=pltpu.PrefetchScalarGridSpec(
            num_scalar_prefetch=1,
            grid=(n,),
            in_specs=[block, block, pl.BlockSpec((rows, 1), lambda i, dests: (0, 0))],
            out_specs=pl.BlockSpec((1, rows, 2 * width), lambda i, dests: (i, 0, 0)),
        ),
        out_shape=jax.ShapeDtypeStruct((n, rows, 2 * width), BF),
    )(dests, w_gate, w_up, gain)


def term_kernel(count, m, spots, *refs):
    lefts, rights = refs[:count], refs[count : 2 * count]
    keep_ref, send_ref, held = refs[2 * count :]
    held[...] = sum(mm_t(z[...], g[...]) for z, g in zip(lefts, rights))
    rows = held.shape[0] // m
    core, side = spots[spots.shape[0] - 2], spots[spots.shape[0] - 1]
    for far in range(m // 2):
        for ref, choice in ((keep_ref, core), (send_ref, 1 - core)):
            owner = 2 * (side ^ far) + choice
            ref[far, 0] = held[pl.ds(pl.multiple_of(owner * rows, rows), rows), :].astype(BF)


def term(m, n, owners, f, lefts, rights):
    count = len(lefts)
    tokens, width = rights[0].shape
    block = lefts[0].shape[1] // n
    if n > 1 and block % 128:
        full = sum(mm_t(z, g) for z, g in zip(lefts, rights)).astype(BF)
        full = full.reshape(n, m // 2, 2, block // m, width)[owners].transpose(1, 2, 0, 3, 4)
        full = full[(f // 2) ^ jnp.arange(m // 2)]
        return pick(full, f % 2, 1), pick(full, 1 - f % 2, 1)
    out = pl.BlockSpec((m // 2, 1, block // m, width), lambda i, spots: (0, i, 0, 0))
    return pl.pallas_call(
        functools.partial(term_kernel, count, m),
        grid_spec=pltpu.PrefetchScalarGridSpec(
            num_scalar_prefetch=1,
            grid=(owners.shape[0],),
            in_specs=[pl.BlockSpec((tokens, block), lambda i, spots: (0, spots[i]))] * count
            + [pl.BlockSpec((tokens, width), lambda i, spots: (0, 0))] * count,
            out_specs=[out, out],
            scratch_shapes=[pltpu.VMEM((block, width), F32)],
        ),
        out_shape=[
            jax.ShapeDtypeStruct((m // 2, owners.shape[0], block // m, width), BF)
        ] * 2,
        compiler_params=pltpu.CompilerParams(vmem_limit_bytes=(24 if n > 1 else 44) << 20),
        cost_estimate=pl.CostEstimate(
            flops=2 * count * tokens * owners.shape[0] * block * width,
            bytes_accessed=2 * owners.shape[0] * block * (count * tokens + width)
            + 2 * count * tokens * width,
            transcendentals=0,
        ),
    )(jnp.concatenate([owners, jnp.stack([f % 2, f // 2])]), *lefts, *rights)


def lanes(width):
    return lax.broadcasted_iota(jnp.int32, (1, width), 1)


def turned(x):
    half = HEAD_DIM // 2
    low = lanes(128) % HEAD_DIM < half
    return jnp.where(low, -pltpu.roll(x, 128 - half, 1), pltpu.roll(x, half, 1))


def in_halves(f, x):
    return jnp.concatenate([f(x[:, i : i + 128]) for i in range(0, x.shape[1], 128)], axis=1)


def fill_pads(heads, kv, row, kpad, vpad):
    width = kpad.shape[2]
    swapped = pltpu.roll(kv, HEAD_DIM, 1)
    first = lanes(128) < HEAD_DIM
    both_k = jnp.where(first, kv, swapped)
    both_v = jnp.where(first, swapped, kv)
    wide_k = jnp.concatenate([both_k] * (width // 128), axis=1)
    wide_v = jnp.concatenate([both_v] * (width // 128), axis=1)
    for h in range(heads):
        own = lanes(width) // HEAD_DIM == h
        kpad[h, row, :] = jnp.where(own, wide_k, 0.0).astype(BF)
        vpad[h, row, :] = jnp.where(own, wide_v, 0.0).astype(BF)


def key_rows(stream, each):
    step = 256

    @pl.loop(0, stream // step)
    def _(i):
        each(pl.ds(pl.multiple_of(i * step, step), step))


def hidden_bias(facts, table):
    seen = (facts[:, 64:65] == table[64:65, :]) & (table[65:66, :] <= facts[:, 65:66])
    return jnp.where(seen, 0.0, HIDE)


def spread_lanes(x):
    x = jnp.where(lanes(128) < 32, x, 0.0)
    x = x + pltpu.roll(x, 32, 1)
    return x + pltpu.roll(x, 64, 1)


def waves(facts):
    return spread_lanes(facts), spread_lanes(pltpu.roll(facts, 96, 1))


def attend_kernel(
    heads, base, act_ref, table_ref, facts_in, o_ref, lse_ref, q_ref, kv_ref, *rest
):
    kpad, vpad = rest[-2:]
    facts_ref = rest[0] if base == 0 else facts_in
    rows, width = q_ref.shape
    stream = act_ref.shape[0]

    @pl.when(pl.program_id(0) == 0)
    def _():
        def each(row):
            if base == 0:
                facts_ref[row, :] = table_ref[:, row].T
            cos, sin = waves(facts_ref[row, :])
            kv = act_ref[row, width : width + 128]
            rot = kv * cos + turned(kv) * sin
            kv = jnp.where(lanes(128) < HEAD_DIM, rot, kv)
            kv_ref[row, :] = kv.astype(BF)
            fill_pads(heads, kv, row, kpad, vpad)

        key_rows(stream, each)

    here = pl.ds(pl.multiple_of(base + pl.program_id(0) * rows, rows), rows)
    facts = facts_ref[here, :]
    cos, sin = waves(facts)
    q = in_halves(lambda x: x * cos + turned(x) * sin, act_ref[here, :width])
    q = (q * (1.0 / math.sqrt(HEAD_DIM))).astype(BF)
    q_ref[...] = q
    bias = hidden_bias(facts, table_ref)
    out = jnp.zeros((rows, width), F32)
    lse = jnp.zeros((rows, 128), F32)
    for h in range(heads):
        s = against(q, kpad[h]) + bias
        top = jnp.max(s, axis=1, keepdims=True)
        p = jnp.exp(s - top)
        total = jnp.sum(p, axis=1, keepdims=True)
        out = out + mm(p.astype(BF), vpad[h]) / total
        lse = jnp.where(lanes(128) == h, top + jnp.log(total), lse)
    o_ref[...] = out.astype(BF)
    lse_ref[...] = lse


def attend_back_kernel(
    heads, base, first, q_ref, g_ref, kv_ref, table_ref, facts_ref, inv_ref, lse_ref, *rest
):
    if first:
        ga_ref, gs_ref, dk_out, dv_out, kpad, vpad, dk, dv = rest
    else:
        dk_in, dv_in, ga_ref, gs_ref, kv_ga, kv_gs, kpad, vpad, dk, dv = rest
    rows, width = q_ref.shape
    stream = kv_ref.shape[0]

    @pl.when(pl.program_id(0) == 0)
    def _():
        key_rows(stream, lambda row: fill_pads(heads, kv_ref[row, :].astype(F32), row, kpad, vpad))
        dk[...] = jnp.zeros_like(dk) if first else dk_in[...]
        dv[...] = jnp.zeros_like(dv) if first else dv_in[...]

    here = pl.ds(pl.multiple_of(base + pl.program_id(0) * rows, rows), rows)
    bias = hidden_bias(facts_ref[here, :], table_ref)
    q = q_ref[...]
    g = g_ref[...]
    dq = jnp.zeros((rows, width), F32)
    for h in range(heads):
        p = jnp.exp(against(q, kpad[h]) + (bias - lse_ref[:, h : h + 1]))
        dp = against(g, vpad[h])
        delta = jnp.sum(p * dp, axis=1, keepdims=True)
        ds = (p * (dp - delta)).astype(BF)
        dq = dq + mm(ds, kpad[h])
        own = lanes(width) // HEAD_DIM == h
        dk[...] += mm_t(ds, jnp.where(own, q, 0).astype(BF))
        dv[...] += mm_t(p.astype(BF), jnp.where(own, g, 0).astype(BF))
    dq = dq * (1.0 / math.sqrt(HEAD_DIM))

    def turn_back(row, x):
        cos, sin = waves(facts_ref[row, :])
        return x * cos - turned(x * sin)

    ga = in_halves(lambda x: turn_back(here, x), dq)
    ga_ref[...] = ga.astype(BF)
    gs_ref[...] = (ga * inv_ref[here, :]).astype(BF)

    @pl.when(pl.program_id(0) == pl.num_programs(0) - 1)
    def _():
        if first:
            dk_out[...] = dk[...]
            dv_out[...] = dv[...]
            return

        def folded(x):
            x = sum(x[:, i : i + 128] for i in range(0, width, 128))
            return x + pltpu.roll(x, HEAD_DIM, 1)

        def each(row):
            gk = turn_back(row, folded(dk[row, :]))
            gkv = jnp.where(lanes(128) < HEAD_DIM, gk, folded(dv[row, :]))
            kv_ga[row, :] = gkv.astype(BF)
            kv_gs[row, :] = (gkv * inv_ref[row, :]).astype(BF)

        key_rows(stream, each)


def attend_specs(rows, stream, base):
    def part(width):
        return pl.BlockSpec((rows, width), lambda i: (i, 0))

    def by_row(width):
        return pl.BlockSpec((rows, width), lambda i: (i + base // rows, 0))

    def whole(width):
        return pl.BlockSpec((stream, width), lambda i: (0, 0))

    return part, by_row, whole


def attend(heads, half, act, table, facts=None):
    stream, width = act.shape
    width, count = width - 128, stream // 2
    base = half * count
    rows = 256 if stream <= 1024 else 128
    part, by_row, whole = attend_specs(rows, stream, base)
    first = half == 0
    return pl.pallas_call(
        functools.partial(attend_kernel, heads, base),
        grid=(count // rows,),
        in_specs=[
            whole(width + 128),
            pl.BlockSpec((128, stream), lambda i: (0, 0)),
            pl.BlockSpec((8, 128), lambda i: (0, 0)) if first else whole(128),
        ],
        out_specs=[part(width), part(128), part(width), whole(128)] + [whole(128)] * first,
        out_shape=[
            jax.ShapeDtypeStruct((count, width), BF),
            jax.ShapeDtypeStruct((count, 128), F32),
            jax.ShapeDtypeStruct((count, width), BF),
            jax.ShapeDtypeStruct((stream, 128), BF),
        ]
        + [jax.ShapeDtypeStruct((stream, 128), F32)] * first,
        scratch_shapes=[pltpu.VMEM((heads, stream, width), BF)] * 2,
        compiler_params=pltpu.CompilerParams(vmem_limit_bytes=28 << 20),
        cost_estimate=pl.CostEstimate(
            flops=4 * stream * count * heads * 256,
            bytes_accessed=8 * stream * width,
            transcendentals=stream * count * heads,
        ),
    )(act, table, jnp.zeros((8, 128), F32) if first else facts)


def attend_back(heads, half, q, g, kv, table, facts, inverse, lse, sums=()):
    count, width = q.shape
    stream = kv.shape[0]
    base = half * count
    rows = 256 if stream <= 1024 else 128
    part, by_row, whole = attend_specs(rows, stream, base)
    first = half == 0
    last_width, last_type = (width, F32) if first else (128, BF)
    return pl.pallas_call(
        functools.partial(attend_back_kernel, heads, base, first),
        grid=(count // rows,),
        in_specs=[
            part(width), part(width), whole(128),
            pl.BlockSpec((128, stream), lambda i: (0, 0)), whole(128), whole(1), part(128),
        ] + [whole(width)] * len(sums),
        out_specs=[part(width)] * 2 + [whole(last_width)] * 2,
        out_shape=[jax.ShapeDtypeStruct((count, width), BF)] * 2
        + [jax.ShapeDtypeStruct((stream, last_width), last_type)] * 2,
        scratch_shapes=[
            *([pltpu.VMEM((heads, stream, width), BF)] * 2),
            *([pltpu.VMEM((stream, width), F32)] * 2),
        ],
        compiler_params=pltpu.CompilerParams(vmem_limit_bytes=32 << 20),
        cost_estimate=pl.CostEstimate(
            flops=10 * stream * count * heads * 256,
            bytes_accessed=20 * stream * width,
            transcendentals=stream * count * heads,
        ),
    )(q, g, kv, table, facts, inverse, lse, *sums)


def finish_ffn_kernel(n, spots, *refs):
    gate_ref, up_ref, gain_ref, og_ref, ou_ref, gg_ref = refs[n:]
    width = gate_ref.shape[1]
    gain = gain_ref[...]
    step = pl.program_id(0)

    @pl.when(step == 0)
    def _():
        gg_ref[...] = jnp.zeros_like(gg_ref)

    for k in range(n):

        @pl.when(step == k)
        def _(piece=refs[k]):
            gate = piece[:, :width].astype(F32)
            up = piece[:, width:].astype(F32)
            og_ref[...] = gate * gain
            ou_ref[...] = up * gain
            term = jnp.sum(
                gate * gate_ref[...].astype(F32) + up * up_ref[...].astype(F32),
                axis=1,
                keepdims=True,
            )
            gg_ref[...] += jnp.broadcast_to(term, gg_ref.shape)


def finish_ffn(pieces, spots, w_gate, w_up, gain):
    n = len(pieces)
    rows, both = pieces[0].shape
    width = both // 2
    block = pl.BlockSpec((rows, width), lambda i, spots: (0, spots[i]))
    return pl.pallas_call(
        functools.partial(finish_ffn_kernel, n),
        grid_spec=pltpu.PrefetchScalarGridSpec(
            num_scalar_prefetch=1,
            grid=(n,),
            in_specs=[pl.BlockSpec((rows, both), lambda i, spots: (0, 0))] * n
            + [block, block, pl.BlockSpec((rows, 1), lambda i, spots: (0, 0))],
            out_specs=[block, block, pl.BlockSpec((rows, 128), lambda i, spots: (0, 0))],
        ),
        out_shape=[
            jax.ShapeDtypeStruct(w_gate.shape, F32),
            jax.ShapeDtypeStruct(w_gate.shape, F32),
            jax.ShapeDtypeStruct((rows, 128), F32),
        ],
        compiler_params=pltpu.CompilerParams(vmem_limit_bytes=24 << 20),
    )(spots, *pieces, w_gate, w_up, gain)


def finish_qkv_kernel(n, spots, pieces, q_ref, k_ref, v_ref, gain_ref, oq, ok, ov, gg_ref):
    q_width = q_ref.shape[1] // n
    sharers = n // KV_HEADS
    gain = gain_ref[...]
    term = jnp.zeros((q_ref.shape[0], 1), F32)
    for kv in range(KV_HEADS):
        held = 0.0
        for j in range(sharers):
            c = kv * sharers + j
            piece = pieces[spots[c]].astype(F32)
            here = slice(c * q_width, (c + 1) * q_width)
            q = piece[:, :q_width]
            held = held + piece[:, q_width:]
            oq[:, here] = q * gain
            term += jnp.sum(q * q_ref[:, here].astype(F32), axis=1, keepdims=True)
        here = slice(kv * HEAD_DIM, (kv + 1) * HEAD_DIM)
        k, v = held[:, :HEAD_DIM], held[:, HEAD_DIM:]
        ok[:, here] = k * gain
        ov[:, here] = v * gain
        term += jnp.sum(
            k * k_ref[:, here].astype(F32) + v * v_ref[:, here].astype(F32), axis=1, keepdims=True
        )
    gg_ref[...] = jnp.broadcast_to(term, gg_ref.shape)


def finish_qkv(pieces, spots, w_query, w_key, w_value, gain):
    n, rows, _ = pieces.shape
    vmem = pl.BlockSpec(memory_space=pltpu.VMEM)
    return pl.pallas_call(
        functools.partial(finish_qkv_kernel, n),
        in_specs=[pl.BlockSpec(memory_space=pltpu.SMEM)] + [vmem] * 5,
        out_specs=[vmem] * 4,
        out_shape=[
            jax.ShapeDtypeStruct(w_query.shape, F32),
            jax.ShapeDtypeStruct(w_key.shape, F32),
            jax.ShapeDtypeStruct(w_value.shape, F32),
            jax.ShapeDtypeStruct((rows, 128), F32),
        ],
    )(spots, pieces, w_query, w_key, w_value, gain)


def norm_back(grad_scaled, unit_rows, inverse):
    return inverse * (
        grad_scaled - unit_rows * jnp.mean(grad_scaled * unit_rows, axis=1, keepdims=True)
    )


def rms_inverse(values):
    return lax.rsqrt(jnp.mean(values * values, axis=1, keepdims=True) + EPSILON)


def body(
    tokens,
    teacher,
    valid_mask,
    lengths,
    span_order,
    w_query,
    w_key,
    w_value,
    w_out,
    w_gate,
    w_up,
    w_down,
    gain_attn,
    gain_ffn,
):
    net = Links()
    n, m, ring = net.n, net.m, net.ring
    x_low = tokens[0]
    tok_rows, width = x_low.shape
    rows = w_query.shape[0]
    heads = HEADS // n
    q_width = heads * HEAD_DIM
    sharers = n // KV_HEADS
    ff_slice = w_gate.shape[1] // n
    stream = tok_rows * n
    spans = tok_rows // SPAN

    jobs, box = net.jobs, net.box

    def later(name, key, job):
        jobs.setdefault(name, {})[key] = job

    def core(x):
        return net.flip(x, "fsdp", 1)

    def side(x):
        return net.flip(x, "fsdp", 2)

    gain_a = gain_attn.astype(F32)[:, None]
    gain_f = gain_ffn.astype(F32)[:, None]
    routes, origins = net.routes(), net.origins()
    pair_moves = [(da, dq) for da in range(ring) for dq in range(2)]
    dests, sources = net.dests(pair_moves), net.sources(pair_moves)
    span_row = jnp.broadcast_to(
        jnp.pad(span_order[0].astype(BF), (0, q_width + 2 * HEAD_DIM - spans))[None, :],
        (16, q_width + 2 * HEAD_DIM),
    )
    straight, across = cut_qkv(n, routes, w_query, w_key, w_value, gain_a, span_row)

    def along(first, other):
        def job(begun):
            ready = tie(jnp.stack([first, box[other]], axis=1), begun)
            return [net.shift(ready[da], da, 0) if da else ready[da] for da in range(ring)]

        return job

    half_rows = w_down.shape[0] // 2
    later("ax0", "q_across", lambda begun: net.shift(across, 0, 1))
    later("ax1", "out_side", lambda begun: side(tie(w_out, begun)))
    later("ax0", "down_side_0", lambda begun: side(w_down[:half_rows]))
    later("ax1", "q_came", along(straight, "q_across"))

    def q_side(begun):
        came = jnp.concatenate(box["q_came"], axis=0)
        return came, side(came)

    later("ax2", "q_sides", q_side)
    later("ax2", "out_core", lambda begun: [core(tie(w_out, begun)), core(box["out_side"])])
    later("ax3", "down_side_1", lambda begun: side(tie(w_down[half_rows:], begun)))
    token_blocks = net.gather_ctx(x_low, "ax")
    q_came, q_other = box["q_sides"]
    qkv_w = net.assemble([[q_came, core(q_came), q_other, core(q_other)]], sources, rows)
    spans_here = tie(q_came, qkv_w)[:, rows, :spans].astype(jnp.int32).reshape(n * spans)
    padding = (-q_width) % 128

    def with_padding(array):
        if not padding:
            return array
        return jnp.concatenate(
            [
                jnp.pad(array[:, :q_width], ((0, 0), (0, padding))),
                array[:, q_width:],
            ],
            axis=1,
        )

    def no_padding(array):
        if not padding:
            return array
        return jnp.concatenate([array[:, :q_width], array[:, q_width + padding :]], axis=1)

    qkv_w = with_padding(qkv_w)
    alone = jnp.zeros((1,), jnp.int32)
    out_w = net.assemble(
        [[x[None] for x in (w_out, box["out_core"][0], box["out_side"], box["out_core"][1])]],
        alone,
        rows,
    )

    direct = net.direct()
    quarter = n // 4
    gate_in, up_in = tie((w_gate, w_up), token_blocks[1][0][0])
    gate_up_cut = cut_ffn(net.dests(direct), gate_in, up_in, gain_f)
    came_ffn = [gate_up_cut[0]]

    def send(pieces, begun, start, stop):
        pieces = tie(pieces, begun)
        return [net.shift(pieces[i], *direct[i]) for i in range(start, stop)]

    place = (
        spans_here[:, None] * SPAN + lax.broadcasted_iota(jnp.int32, (n * spans, SPAN), 1)
    ).reshape(stream)
    seq_ends = jnp.cumsum(lengths[0])
    passed = seq_ends[None, :] <= place[:, None]
    segment = jnp.sum(passed.astype(jnp.int32), axis=1)
    seq_begin = jnp.sum(jnp.where(passed, lengths[0][None, :], 0), axis=1)
    rates = jnp.asarray(rope_rates(HEAD_DIM)[: HEAD_DIM // 2])
    angles = rates[:, None] * (place - seq_begin).astype(F32)[None, :]
    table = jnp.concatenate(
        [
            jnp.cos(angles),
            jnp.sin(angles),
            segment.astype(F32)[None, :],
            place.astype(F32)[None, :],
            jnp.zeros((128 - 66, stream), F32),
        ],
        axis=0,
    )

    x_pairs, inverses, acts_attn = [], [], []
    pair_rows = 2 * tok_rows
    for r in range(ring):
        x_pair = paired(token_blocks[r])
        inverse = rms_inverse(x_pair.astype(F32))
        x_pairs.append(x_pair)
        inverses.append(inverse)
        acts_attn.append(mm(x_pair, qkv_w) * inverse)
    inverse_all = jnp.concatenate(inverses, axis=0)
    act_all = jnp.concatenate(acts_attn, axis=0)
    cuts = [1, max(1, 0 * n // 8), 4 * n // 8, 6 * n // 8, 7 * n // 8, n]
    first = attend(heads, 0, act_all, table)
    sent = send(gate_up_cut, qkv_w, cuts[1], cuts[2])
    act_all, sent = lax.optimization_barrier((act_all, sent))
    came_ffn += sent
    facts = first[4]
    second = attend(heads, 1, act_all, table, facts)
    kv_rot = second[3]
    attended_halves = first[0], second[0]

    def split_pair(block):
        return block[:tok_rows], block[tok_rows:]

    def pair_of(array, r):
        return array[r * pair_rows : (r + 1) * pair_rows]

    inputs = x_low.astype(F32)

    def of_halves(halves, r):
        which, start = divmod(r * pair_rows, stream // 2)
        return halves[which][start : start + pair_rows]

    for i in range(3):
        later(f"ro{i}", f"f_{i}", lambda begun, i=i: send(gate_up_cut, begun, cuts[2 + i], cuts[3 + i]))
    for g in range(4):

        def g_side(begun, g=g):
            pieces = came_ffn + sum((box[f"f_{i}"] for i in range(g)), [])
            block = tie(jnp.stack(pieces[g * quarter : (g + 1) * quarter]), begun)
            return block, side(block)

        def g_core(begun, g=g):
            return [core(x) for x in box[f"g_side{g}"]]

        later(f"ro{g}", f"g_side{g}", g_side)
        later(f"ro{g + 1}" if g < 3 else "ff0", f"g_core{g}", g_core)
    later("ro0", "down_core", lambda begun: core(tie(w_down, begun)))

    def down_far(begun):
        return core(jnp.concatenate([box["down_side_0"], box["down_side_1"]], axis=0))

    later("ff0", "down_far", down_far)
    middle = inputs + net.scatter_ctx(
        lambda r: split_pair(mm(of_halves(attended_halves, r)[:, :q_width], out_w)), "ro"
    )

    inverse_ffn = rms_inverse(middle)
    unit_ffn = middle * inverse_ffn
    unit_blocks = net.gather_ctx(unit_ffn.astype(BF), "ff")
    gate_up_w = net.assemble(
        [
            [box[f"g_side{g}"][0], box[f"g_core{g}"][0], box[f"g_side{g}"][1], box[f"g_core{g}"][1]]
            for g in range(4)
        ],
        net.sources(direct),
        rows,
    )
    down_sides = jnp.concatenate([box["down_side_0"], box["down_side_1"]], axis=0)
    down_w = net.assemble(
        [[x[None] for x in (w_down, box["down_core"], down_sides, box["down_far"])]],
        alone,
        w_down.shape[0],
    )
    z_pairs = [paired(blocks) for blocks in unit_blocks]
    acts, hiddens = {}, {}

    def down_part(r):
        both = mm(z_pairs[r], gate_up_w)
        gate, up = both[:, :ff_slice], both[:, ff_slice:]
        acts[r] = (gate, up)
        hiddens[r] = (gate * jax.nn.sigmoid(gate) * up).astype(BF)
        return split_pair(mm(hiddens[r], down_w))

    out_full = middle + net.scatter_ctx(down_part, "fo")

    valid_f = valid_mask[0].astype(F32)[:, None]
    missed = (out_full - teacher[0].astype(F32)) * valid_f
    sums = jnp.stack([jnp.sum(missed * missed), jnp.sum(valid_f)]).reshape(1, 2)
    grad_out = missed

    grad_blocks = net.gather_ctx(grad_out.astype(BF), "bf")
    grad_pairs = [paired(blocks) for blocks in grad_blocks]
    grad_acts = {}

    def unit_part(r):
        gate, up = acts[r]
        grad_hidden = against(grad_pairs[r], down_w)
        share = jax.nn.sigmoid(gate)
        grad_gate = grad_hidden * up * share * (1.0 + gate * (1.0 - share))
        grad_up = grad_hidden * (gate * share)
        grad_acts[r] = jnp.concatenate([grad_gate.astype(BF), grad_up.astype(BF)], axis=1)
        return split_pair(against(grad_acts[r], gate_up_w))

    owners = net.dests(direct)
    term_slots = ["bo2", "bo3", "am0", "am1", "am2", "am3", "ar0"]

    def listed(items):
        return [items[r] for r in range(ring)]

    for g in range(4):

        def g_term(begun, g=g):
            lefts, rights = tie((z_pairs, listed(grad_acts)), begun)
            return term(m, n, owners[g * quarter : (g + 1) * quarter], net.f, lefts, rights)

        def g_cross(begun, g=g):
            return core(box[f"t{g}"][1])

        def g_far(begun, g=g):
            keep, got = box[f"t{g}"][0], box[f"tc{g}"]
            return side((keep[1].astype(F32) + got[1]).astype(BF))

        later(term_slots[g], f"t{g}", g_term)
        later(term_slots[g + 1], f"tc{g}", g_cross)
        later(term_slots[g + 2], f"ts{g}", g_far)

    def d_term(begun):
        lefts, rights = tie((listed(hiddens), grad_pairs), begun)
        return term(m, 1, alone, net.f, lefts, rights)

    later("am2", "d", d_term)
    later("am3", "dc", lambda begun: core(box["d"][1]))

    def d_far(begun):
        block = (tie(box["d"][0], begun)[1, 0].astype(F32) + box["dc"][1, 0]).astype(BF)
        return block[half_rows:], side(block[:half_rows])


    axes = [("ctx", 1 << i) for i in range((n - 1).bit_length())]
    axes += [("fsdp", 1 << i) for i in range((m - 1).bit_length())]
    spots = [f"am{r}" for r in range(ring)] + [f"ar{r}" for r in range(ring)]
    box["sums"] = sums
    for name, (axis, bit) in zip(spots, axes):
        later(name, "sums", lambda begun, a=axis, b=bit: box["sums"] + net.flip(tie(box["sums"], begun), a, b))

    unit_parts = {r: unit_part(r) for r in net.scatter_order()}
    grad_unit = net.scatter_ctx(unit_parts.get, "bo")
    grad_middle = grad_out + norm_back(grad_unit, unit_ffn, inverse_ffn)
    middle_low = grad_middle.astype(BF)

    middle_blocks = net.gather_ctx(middle_low, "am")
    middle_pairs = [paired(blocks) for blocks in middle_blocks]

    def summed(i):
        g, at = divmod(i, quarter)
        keep, got, far = box[f"t{g}"][0], box[f"tc{g}"], box[f"ts{g}"]
        return (keep[0, at].astype(F32) + got[0, at] + far[at]).astype(BF)

    def send_sum(begun, start, stop):
        return [net.shift(tie(summed(i), begun), *direct[i]) for i in range(start, stop)]

    def back_half(half):
        parts = [
            against(middle_pairs[r], out_w).astype(BF)
            for r in range(half * ring // 2, (half + 1) * ring // 2)
        ]
        grads = jnp.concatenate(parts, axis=0)
        return jnp.pad(grads, ((0, 0), (0, padding))) if padding else grads

    grads_first, grads_second = back_half(0), back_half(1)
    came_sums = [summed(0)]
    cuts = [1, 3 * n // 8, 5 * n // 8, 7 * n // 8, n]
    sent = send_sum(middle_blocks[-1][0][0], cuts[0], cuts[1])
    grads_first, grads_second, sent = lax.optimization_barrier((grads_first, grads_second, sent))
    came_sums += sent
    fixed = kv_rot, table, facts, inverse_all
    sent, box["ds0"] = send_sum(grads_first, cuts[1], cuts[2]), d_far(grads_first)
    backed = attend_back(heads, 0, first[2], grads_first, *fixed, first[1])
    backed, grads_second, sent, box["ds0"] = lax.optimization_barrier(
        (backed, grads_second, sent, box["ds0"])
    )
    came_sums += sent
    gq_first, gs_first, sum_k, sum_v = backed
    sent = send_sum(grads_second, cuts[2], cuts[3])
    box["ds1"] = side(tie(box["ds0"][0], grads_second))
    backed = attend_back(heads, 1, second[2], grads_second, *fixed, second[1], (sum_k, sum_v))
    (gq_second, gs_second, g_kv, gs_kv), sent, box["ds1"] = lax.optimization_barrier(
        (backed, sent, box["ds1"])
    )
    came_sums += sent

    def attn_part(r):
        rows_q = of_halves((gq_first, gq_second), r)
        grads = jnp.concatenate([rows_q, pair_of(g_kv, r)], axis=1)
        return split_pair(against(grads, qkv_w))

    def q_term(begun):
        grads = [
            jnp.concatenate([of_halves((gs_first, gs_second), r), pair_of(gs_kv, r)], axis=1)
            for r in range(ring)
        ]
        lefts, grads = tie((x_pairs, grads), begun)
        return term(m, n, dests, net.f, lefts, grads)

    def q_back(begun):
        (keep, _), got = box["qt"], box["qc"]
        block = keep[0].astype(F32) + got[0] + box["qs"]
        if padding:
            block = jnp.concatenate([block[..., :q_width], block[..., q_width + padding :]], axis=2)
        block = block.astype(BF).reshape(ring, 2, rows, q_width + 2 * HEAD_DIM)
        return block[:, 0], net.shift(block[:, 1], 0, 1)

    def q_along(begun):
        ready = tie(jnp.stack(box["qb"], axis=1), begun)
        return [net.shift(ready[da], da, 0) if da else ready[da] for da in range(ring)]

    def o_term(begun):
        lefts = [of_halves(attended_halves, r)[:, :q_width] for r in range(ring)]
        lefts, grads = tie((lefts, middle_pairs), begun)
        return term(m, 1, alone, net.f, lefts, grads)

    def crossed(key, made):
        return lambda begun: core(tie(box[made][1], begun))

    def farther(made, got):
        return lambda begun: side((box[made][0][1].astype(F32) + box[got][1]).astype(BF))

    def ends(begun):
        square_sum, valid_count = box["sums"][0, 0], box["sums"][0, 1]
        box["loss"] = 0.5 * square_sum / (width * valid_count)
        box["spread"] = (tok_rows * n * m) / valid_count
        pieces = tie(came_sums + box["c_last"], begun)
        return finish_ffn(pieces, net.sources(direct), w_gate, w_up, gain_f * box["spread"])

    later("ar0", "ot", o_term)
    later("ar0", "qt", q_term)
    later("ar0", "c_last", lambda begun: send_sum(begun, cuts[3], n))
    later("ar1", "qc", crossed("qc", "qt"))
    later("ar1", "oc", crossed("oc", "ot"))
    later("ar2", "qs", farther("qt", "qc"))
    later("ar2", "os", farther("ot", "oc"))
    later("ar3", "qb", q_back)
    later(f"ar{max(2, len(axes) - ring)}", "ffn", ends)
    grad_attn = net.scatter_ctx(attn_part, "ar")
    spread = box["spread"]
    inverse_attn = rms_inverse(inputs)
    grad_input = grad_middle + norm_back(grad_attn, inputs * inverse_attn, inverse_attn)
    grad_w_query, grad_w_key, grad_w_value, gain_sum_attn = finish_qkv(
        jnp.concatenate(q_along(grad_attn), axis=0), origins, w_query, w_key, w_value, gain_a * spread
    )
    grad_w_out = (box["ot"][0][0, 0].astype(F32) + box["oc"][0, 0] + box["os"][0]) * spread
    down_keep = box["d"][0][0, 0].astype(F32) + box["dc"][0, 0]
    down_far = jnp.concatenate([box["ds0"][1], box["ds1"]], axis=0)
    grad_down = down_keep + down_far
    grad_w_gate, grad_w_up, gain_sum_ffn = box["ffn"]
    loss_value = box["loss"]
    return (
        out_full.astype(BF)[None],
        loss_value,
        (grad_input * spread)[None],
        grad_w_query,
        grad_w_key,
        grad_w_value,
        grad_w_out,
        grad_w_gate,
        grad_w_up,
        grad_down * spread,
        gain_sum_attn[:, 0] * spread,
        gain_sum_ffn[:, 0] * spread,
    )


def solution(mesh):
    token_spec = P("fsdp", "ctx", None)
    row_spec = P(("ctx", "fsdp"), None)
    gain_spec = P(("ctx", "fsdp"))
    in_specs = (
        token_spec,
        token_spec,
        P("fsdp", "ctx"),
        P("fsdp", None),
        P("fsdp", "ctx"),
        *([row_spec] * 7),
        gain_spec,
        gain_spec,
    )
    out_specs = (token_spec, P(), token_spec, *([row_spec] * 7), gain_spec, gain_spec)
    return jax.shard_map(body, mesh=mesh, in_specs=in_specs, out_specs=out_specs, check_vma=False)
```

```python
import functools
import math

import jax
import jax.numpy as jnp
import numpy as np
from jax import lax
from jax.experimental import pallas as pl
from jax.experimental.pallas import tpu as pltpu
from jax.sharding import PartitionSpec as P

HEADS = 32
KV_HEADS = 8
HEAD_DIM = 64
SPAN = 128
EPSILON = 1e-05
HIDE = -1e30
TWICE = ("bf", "bo")
BF = jnp.bfloat16
F32 = jnp.float32


def rope_rates(head_width):
    frequency = 1.0 / 500000.0 ** (np.arange(0, head_width, 2) / head_width)
    wavelength = 2.0 * np.pi / frequency
    blend_share = (8192.0 / wavelength - 1.0) / 3.0
    blended = (1.0 - blend_share) * frequency / 32.0 + blend_share * frequency
    frequency = np.where(
        wavelength < 2048.0, frequency, np.where(wavelength > 8192.0, frequency / 32.0, blended)
    )
    return np.concatenate([frequency, frequency]).astype(np.float32)


def mm(left, right):
    return jnp.dot(left, right, preferred_element_type=F32)


def mm_t(left, right):
    return lax.dot_general(left, right, (((0,), (0,)), ((), ())), preferred_element_type=F32)


def against(left, right):
    return lax.dot_general(left, right, (((1,), (1,)), ((), ())), preferred_element_type=F32)


def pick(array, index, axis=0):
    return lax.dynamic_index_in_dim(array, index, axis, keepdims=False)


def paired(blocks):
    rows = [jnp.concatenate(pieces, axis=1) if len(pieces) > 1 else pieces[0] for pieces in blocks]
    return jnp.concatenate(rows, axis=0)


def tie(value, *others):
    return lax.optimization_barrier((value, *others))[0]


class Links:
    def __init__(self):
        self.n = lax.axis_size("ctx")
        self.m = lax.axis_size("fsdp")
        self.ring = self.n // 2
        self.c = lax.axis_index("ctx")
        self.f = lax.axis_index("fsdp")
        self.a = self.c // 2
        self.b = self.c % 2
        self.box, self.jobs = {}, {}

    def shift(self, x, da, dq):
        perm = [
            (a * 2 + b, ((a + da) % self.ring) * 2 + (b ^ dq))
            for a in range(self.ring)
            for b in range(2)
        ]
        return lax.ppermute(x, "ctx", perm)

    def flip(self, x, axis, bit):
        size = self.n if axis == "ctx" else self.m
        return lax.ppermute(x, axis, [(i, i ^ bit) for i in range(size)])

    def slot(self, name, begun, mains):
        made = {key: job(begun) for key, job in self.jobs.pop(name, {}).items()}
        mains, made = lax.optimization_barrier((mains, made))
        self.box.update(made)
        return mains

    def cut(self, x, name):
        count = 2 if name in TWICE else 1
        step = x.shape[1] // count
        return [x[:, i * step : (i + 1) * step] for i in range(count)]

    def gather_ctx(self, x, name):
        out = []
        held = self.cut(x, name)
        for r in range(self.ring):
            pairs, moved = [], []
            for i, piece in enumerate(held):
                mains = [self.shift(piece, 0, 1)]
                if r < self.ring - 1:
                    mains.append(self.shift(piece, 1, 0))
                last = i == len(held) - 1
                mains = self.slot(f"{name}{r}" if last else "", piece, mains)
                pairs.append(mains[0])
                moved.append(mains[-1])
            out.append((held, pairs))
            held = moved
        return out

    def scatter_order(self):
        return list(range(1, self.ring)) + [0]

    def scatter_ctx(self, part, name):
        count = len(self.cut(jnp.zeros((1, 2)), name))
        held, got = [None] * count, [None] * count
        for i, r in enumerate(self.scatter_order()):
            mine, other = part(r)
            pieces = zip(self.cut(mine, name), self.cut(other.astype(BF), name))
            for k, (own, away) in enumerate(pieces):
                if i:
                    away = tie(away, got[k])
                mains = [self.shift(away, 0, 1)]
                if i:
                    mains.append(self.shift(held[k].astype(BF), 1, 0))
                mains = self.slot(f"{name}{i}" if k == count - 1 else "", away, mains)
                got[k] = mains[0]
                held[k] = own + sum(block.astype(F32) for block in mains)
        return held[0] if count == 1 else jnp.concatenate(held, axis=1)

    def direct(self):
        near = sorted(range(1, self.ring), key=lambda da: (min(da, self.ring - da), da))
        return [(0, 0)] + [(da, 0) for da in near] + [(0, 1)] + [(da, 1) for da in near]

    def dests(self, moves):
        spots = [((self.a + da) % self.ring) * 2 + (self.b ^ dq) for da, dq in moves]
        return jnp.stack(spots).astype(jnp.int32)

    def sources(self, moves):
        return self.dests([((self.ring - da) % self.ring, dq) for da, dq in moves])

    def routes(self):
        c = jnp.arange(self.n, dtype=jnp.int32)
        return ((c // 2 + self.ring - self.a) % self.ring) * 2 + (self.b ^ (c % 2))

    def origins(self):
        c = jnp.arange(self.n, dtype=jnp.int32)
        return ((self.a + self.ring - c // 2) % self.ring) * 2 + (self.b ^ (c % 2))

    def assemble(self, groups, spots, rows):
        sizes = [group[0].shape[0] for group in groups]
        count = sum(sizes)
        held_rows, width = groups[0][0].shape[1:]
        parts = max(1, min(width // 256, 8 // count))
        part = width // parts
        marks = self.f ^ jnp.arange(self.m, dtype=jnp.int32)
        specs, base = [], 0
        for size in sizes:

            def at(i, j, spots, base=base, size=size):
                return jnp.clip(i - base, 0, size - 1), 0, j

            specs += [pl.BlockSpec((1, held_rows, part), at)] * self.m
            base += size
        out = pl.pallas_call(
            functools.partial(place_kernel, sizes, self.m),
            grid_spec=pltpu.PrefetchScalarGridSpec(
                num_scalar_prefetch=1,
                grid=(count, parts),
                in_specs=specs,
                out_specs=pl.BlockSpec(
                    (1, self.m, rows, part), lambda i, j, spots: (spots[i], 0, 0, j)
                ),
            ),
            out_shape=jax.ShapeDtypeStruct((count, self.m, rows, width), BF),
            compiler_params=pltpu.CompilerParams(vmem_limit_bytes=24 << 20),
            cost_estimate=pl.CostEstimate(
                flops=0, bytes_accessed=4 * count * self.m * rows * width, transcendentals=0
            ),
        )(jnp.concatenate([spots, marks]), *[block for group in groups for block in group])
        return out.reshape(count * self.m * rows, width)


def place_kernel(sizes, m, spots, *refs):
    count = sum(sizes)
    out = refs[-1]
    base = 0
    for g, size in enumerate(sizes):

        @pl.when((pl.program_id(0) >= base) & (pl.program_id(0) < base + size))
        def _(g=g):
            for k in range(m):
                out[0, spots[count + k]] = refs[g * m + k][0, : out.shape[2]]

        base += size


def cut_qkv_kernel(n, spots, q_ref, k_ref, v_ref, gain_ref, span_ref, straight, across):
    rows = q_ref.shape[0]
    q_width = q_ref.shape[1] // n
    sharers = n // KV_HEADS
    gain = gain_ref[...]

    def folded(ref, i, width):
        return (ref[:, i * width : (i + 1) * width].astype(F32) * gain).astype(BF)

    for c in range(n):
        kv = c // sharers
        piece = jnp.concatenate(
            [
                folded(q_ref, c, q_width),
                folded(k_ref, kv, HEAD_DIM),
                folded(v_ref, kv, HEAD_DIM),
            ],
            axis=1,
        )
        move = spots[c]

        def fill(ref, piece=piece, move=move):
            ref[move // 2, :rows, :] = piece
            ref[move // 2, rows:, :] = jnp.broadcast_to(
                span_ref[0:16, : piece.shape[1]], (16, piece.shape[1])
            )

        pl.when(move % 2 == 0)(functools.partial(fill, straight))
        pl.when(move % 2 == 1)(functools.partial(fill, across))


def cut_qkv(n, spots, w_query, w_key, w_value, gain, span):
    rows = w_query.shape[0]
    width = w_query.shape[1] // n + 2 * HEAD_DIM
    vmem = pl.BlockSpec(memory_space=pltpu.VMEM)
    return pl.pallas_call(
        functools.partial(cut_qkv_kernel, n),
        in_specs=[pl.BlockSpec(memory_space=pltpu.SMEM)] + [vmem] * 5,
        out_specs=[vmem] * 2,
        out_shape=[jax.ShapeDtypeStruct((n // 2, rows + 16, width), BF)] * 2,
    )(spots, w_query, w_key, w_value, gain, span)


def cut_ffn_kernel(spots, gate, up, gain_ref, out):
    gain = gain_ref[...]
    width = gate.shape[1]
    out[0, :, :width] = (gate[...].astype(F32) * gain).astype(BF)
    out[0, :, width:] = (up[...].astype(F32) * gain).astype(BF)


def cut_ffn(dests, w_gate, w_up, gain):
    n = dests.shape[0]
    rows, width = w_gate.shape[0], w_gate.shape[1] // n
    block = pl.BlockSpec((rows, width), lambda i, dests: (0, dests[i]))
    return pl.pallas_call(
        cut_ffn_kernel,
        grid_spec=pltpu.PrefetchScalarGridSpec(
            num_scalar_prefetch=1,
            grid=(n,),
            in_specs=[block, block, pl.BlockSpec((rows, 1), lambda i, dests: (0, 0))],
            out_specs=pl.BlockSpec((1, rows, 2 * width), lambda i, dests: (i, 0, 0)),
        ),
        out_shape=jax.ShapeDtypeStruct((n, rows, 2 * width), BF),
    )(dests, w_gate, w_up, gain)


def term_kernel(count, m, spots, *refs):
    lefts, rights = refs[:count], refs[count : 2 * count]
    keep_ref, send_ref, held = refs[2 * count :]
    held[...] = sum(mm_t(z[...], g[...]) for z, g in zip(lefts, rights))
    rows = held.shape[0] // m
    core, side = spots[spots.shape[0] - 2], spots[spots.shape[0] - 1]
    for far in range(m // 2):
        for ref, choice in ((keep_ref, core), (send_ref, 1 - core)):
            owner = 2 * (side ^ far) + choice
            ref[far, 0] = held[pl.ds(pl.multiple_of(owner * rows, rows), rows), :].astype(BF)


def term(m, n, owners, f, lefts, rights):
    count = len(lefts)
    tokens, width = rights[0].shape
    block = lefts[0].shape[1] // n
    if n > 1 and block % 128:
        full = sum(mm_t(z, g) for z, g in zip(lefts, rights)).astype(BF)
        full = full.reshape(n, m // 2, 2, block // m, width)[owners].transpose(1, 2, 0, 3, 4)
        full = full[(f // 2) ^ jnp.arange(m // 2)]
        return pick(full, f % 2, 1), pick(full, 1 - f % 2, 1)
    out = pl.BlockSpec((m // 2, 1, block // m, width), lambda i, spots: (0, i, 0, 0))
    return pl.pallas_call(
        functools.partial(term_kernel, count, m),
        grid_spec=pltpu.PrefetchScalarGridSpec(
            num_scalar_prefetch=1,
            grid=(owners.shape[0],),
            in_specs=[pl.BlockSpec((tokens, block), lambda i, spots: (0, spots[i]))] * count
            + [pl.BlockSpec((tokens, width), lambda i, spots: (0, 0))] * count,
            out_specs=[out, out],
            scratch_shapes=[pltpu.VMEM((block, width), F32)],
        ),
        out_shape=[
            jax.ShapeDtypeStruct((m // 2, owners.shape[0], block // m, width), BF)
        ] * 2,
        compiler_params=pltpu.CompilerParams(vmem_limit_bytes=(24 if n > 1 else 44) << 20),
        cost_estimate=pl.CostEstimate(
            flops=2 * count * tokens * owners.shape[0] * block * width,
            bytes_accessed=2 * owners.shape[0] * block * (count * tokens + width)
            + 2 * count * tokens * width,
            transcendentals=0,
        ),
    )(jnp.concatenate([owners, jnp.stack([f % 2, f // 2])]), *lefts, *rights)


def lanes(width):
    return lax.broadcasted_iota(jnp.int32, (1, width), 1)


def turned(x):
    half = HEAD_DIM // 2
    low = lanes(128) % HEAD_DIM < half
    return jnp.where(low, -pltpu.roll(x, 128 - half, 1), pltpu.roll(x, half, 1))


def in_halves(f, x):
    return jnp.concatenate([f(x[:, i : i + 128]) for i in range(0, x.shape[1], 128)], axis=1)


def fill_pads(heads, kv, row, kpad, vpad):
    width = kpad.shape[2]
    swapped = pltpu.roll(kv, HEAD_DIM, 1)
    first = lanes(128) < HEAD_DIM
    both_k = jnp.where(first, kv, swapped)
    both_v = jnp.where(first, swapped, kv)
    wide_k = jnp.concatenate([both_k] * (width // 128), axis=1)
    wide_v = jnp.concatenate([both_v] * (width // 128), axis=1)
    for h in range(heads):
        own = lanes(width) // HEAD_DIM == h
        kpad[h, row, :] = jnp.where(own, wide_k, 0.0).astype(BF)
        vpad[h, row, :] = jnp.where(own, wide_v, 0.0).astype(BF)


def key_rows(stream, each):
    step = 256

    @pl.loop(0, stream // step)
    def _(i):
        each(pl.ds(pl.multiple_of(i * step, step), step))


def hidden_bias(facts, table):
    seen = (facts[:, 64:65] == table[64:65, :]) & (table[65:66, :] <= facts[:, 65:66])
    return jnp.where(seen, 0.0, HIDE)


def spread_lanes(x):
    x = jnp.where(lanes(128) < 32, x, 0.0)
    x = x + pltpu.roll(x, 32, 1)
    return x + pltpu.roll(x, 64, 1)


def waves(facts):
    return spread_lanes(facts), spread_lanes(pltpu.roll(facts, 96, 1))


def attend_kernel(
    heads, base, act_ref, table_ref, facts_in, o_ref, lse_ref, q_ref, kv_ref, *rest
):
    kpad, vpad = rest[-2:]
    facts_ref = rest[0] if base == 0 else facts_in
    rows, width = q_ref.shape
    stream = act_ref.shape[0]

    @pl.when(pl.program_id(0) == 0)
    def _():
        def each(row):
            if base == 0:
                facts_ref[row, :] = table_ref[:, row].T
            cos, sin = waves(facts_ref[row, :])
            kv = act_ref[row, width : width + 128]
            rot = kv * cos + turned(kv) * sin
            kv = jnp.where(lanes(128) < HEAD_DIM, rot, kv)
            kv_ref[row, :] = kv.astype(BF)
            fill_pads(heads, kv, row, kpad, vpad)

        key_rows(stream, each)

    here = pl.ds(pl.multiple_of(base + pl.program_id(0) * rows, rows), rows)
    facts = facts_ref[here, :]
    cos, sin = waves(facts)
    q = in_halves(lambda x: x * cos + turned(x) * sin, act_ref[here, :width])
    q = (q * (1.0 / math.sqrt(HEAD_DIM))).astype(BF)
    q_ref[...] = q
    bias = hidden_bias(facts, table_ref)
    out = jnp.zeros((rows, width), F32)
    lse = jnp.zeros((rows, 128), F32)
    for h in range(heads):
        s = against(q, kpad[h]) + bias
        top = jnp.max(s, axis=1, keepdims=True)
        p = jnp.exp(s - top)
        total = jnp.sum(p, axis=1, keepdims=True)
        out = out + mm(p.astype(BF), vpad[h]) / total
        lse = jnp.where(lanes(128) == h, top + jnp.log(total), lse)
    o_ref[...] = out.astype(BF)
    lse_ref[...] = lse


def attend_back_kernel(
    heads, base, first, q_ref, g_ref, kv_ref, table_ref, facts_ref, inv_ref, lse_ref, *rest
):
    if first:
        ga_ref, gs_ref, dk_out, dv_out, kpad, vpad, dk, dv = rest
    else:
        dk_in, dv_in, ga_ref, gs_ref, kv_ga, kv_gs, kpad, vpad, dk, dv = rest
    rows, width = q_ref.shape
    stream = kv_ref.shape[0]

    @pl.when(pl.program_id(0) == 0)
    def _():
        key_rows(stream, lambda row: fill_pads(heads, kv_ref[row, :].astype(F32), row, kpad, vpad))
        dk[...] = jnp.zeros_like(dk) if first else dk_in[...]
        dv[...] = jnp.zeros_like(dv) if first else dv_in[...]

    here = pl.ds(pl.multiple_of(base + pl.program_id(0) * rows, rows), rows)
    bias = hidden_bias(facts_ref[here, :], table_ref)
    q = q_ref[...]
    g = g_ref[...]
    dq = jnp.zeros((rows, width), F32)
    for h in range(heads):
        p = jnp.exp(against(q, kpad[h]) + (bias - lse_ref[:, h : h + 1]))
        dp = against(g, vpad[h])
        delta = jnp.sum(p * dp, axis=1, keepdims=True)
        ds = (p * (dp - delta)).astype(BF)
        dq = dq + mm(ds, kpad[h])
        own = lanes(width) // HEAD_DIM == h
        dk[...] += mm_t(ds, jnp.where(own, q, 0).astype(BF))
        dv[...] += mm_t(p.astype(BF), jnp.where(own, g, 0).astype(BF))
    dq = dq * (1.0 / math.sqrt(HEAD_DIM))

    def turn_back(row, x):
        cos, sin = waves(facts_ref[row, :])
        return x * cos - turned(x * sin)

    ga = in_halves(lambda x: turn_back(here, x), dq)
    ga_ref[...] = ga.astype(BF)
    gs_ref[...] = (ga * inv_ref[here, :]).astype(BF)

    @pl.when(pl.program_id(0) == pl.num_programs(0) - 1)
    def _():
        if first:
            dk_out[...] = dk[...]
            dv_out[...] = dv[...]
            return

        def folded(x):
            x = sum(x[:, i : i + 128] for i in range(0, width, 128))
            return x + pltpu.roll(x, HEAD_DIM, 1)

        def each(row):
            gk = turn_back(row, folded(dk[row, :]))
            gkv = jnp.where(lanes(128) < HEAD_DIM, gk, folded(dv[row, :]))
            kv_ga[row, :] = gkv.astype(BF)
            kv_gs[row, :] = (gkv * inv_ref[row, :]).astype(BF)

        key_rows(stream, each)


def attend_specs(rows, stream, base):
    def part(width):
        return pl.BlockSpec((rows, width), lambda i: (i, 0))

    def by_row(width):
        return pl.BlockSpec((rows, width), lambda i: (i + base // rows, 0))

    def whole(width):
        return pl.BlockSpec((stream, width), lambda i: (0, 0))

    return part, by_row, whole


def attend(heads, half, act, table, facts=None):
    stream, width = act.shape
    width, count = width - 128, stream // 2
    base = half * count
    rows = 512 if stream <= 1024 else 128
    part, by_row, whole = attend_specs(rows, stream, base)
    first = half == 0
    return pl.pallas_call(
        functools.partial(attend_kernel, heads, base),
        grid=(count // rows,),
        in_specs=[
            whole(width + 128),
            pl.BlockSpec((128, stream), lambda i: (0, 0)),
            pl.BlockSpec((8, 128), lambda i: (0, 0)) if first else whole(128),
        ],
        out_specs=[part(width), part(128), part(width), whole(128)] + [whole(128)] * first,
        out_shape=[
            jax.ShapeDtypeStruct((count, width), BF),
            jax.ShapeDtypeStruct((count, 128), F32),
            jax.ShapeDtypeStruct((count, width), BF),
            jax.ShapeDtypeStruct((stream, 128), BF),
        ]
        + [jax.ShapeDtypeStruct((stream, 128), F32)] * first,
        scratch_shapes=[pltpu.VMEM((heads, stream, width), BF)] * 2,
        compiler_params=pltpu.CompilerParams(vmem_limit_bytes=28 << 20),
        cost_estimate=pl.CostEstimate(
            flops=4 * stream * count * heads * 256,
            bytes_accessed=8 * stream * width,
            transcendentals=stream * count * heads,
        ),
    )(act, table, jnp.zeros((8, 128), F32) if first else facts)


def attend_back(heads, half, q, g, kv, table, facts, inverse, lse, sums=()):
    count, width = q.shape
    stream = kv.shape[0]
    base = half * count
    rows = 256 if stream <= 1024 else 128
    part, by_row, whole = attend_specs(rows, stream, base)
    first = half == 0
    last_width, last_type = (width, F32) if first else (128, BF)
    return pl.pallas_call(
        functools.partial(attend_back_kernel, heads, base, first),
        grid=(count // rows,),
        in_specs=[
            part(width), part(width), whole(128),
            pl.BlockSpec((128, stream), lambda i: (0, 0)), whole(128), whole(1), part(128),
        ] + [whole(width)] * len(sums),
        out_specs=[part(width)] * 2 + [whole(last_width)] * 2,
        out_shape=[jax.ShapeDtypeStruct((count, width), BF)] * 2
        + [jax.ShapeDtypeStruct((stream, last_width), last_type)] * 2,
        scratch_shapes=[
            *([pltpu.VMEM((heads, stream, width), BF)] * 2),
            *([pltpu.VMEM((stream, width), F32)] * 2),
        ],
        compiler_params=pltpu.CompilerParams(vmem_limit_bytes=32 << 20),
        cost_estimate=pl.CostEstimate(
            flops=10 * stream * count * heads * 256,
            bytes_accessed=20 * stream * width,
            transcendentals=stream * count * heads,
        ),
    )(q, g, kv, table, facts, inverse, lse, *sums)


def finish_ffn_kernel(n, spots, *refs):
    gate_ref, up_ref, gain_ref, og_ref, ou_ref, gg_ref = refs[n:]
    width = gate_ref.shape[1]
    gain = gain_ref[...]
    step = pl.program_id(0)

    @pl.when(step == 0)
    def _():
        gg_ref[...] = jnp.zeros_like(gg_ref)

    for k in range(n):

        @pl.when(step == k)
        def _(piece=refs[k]):
            gate = piece[:, :width].astype(F32)
            up = piece[:, width:].astype(F32)
            og_ref[...] = gate * gain
            ou_ref[...] = up * gain
            term = jnp.sum(
                gate * gate_ref[...].astype(F32) + up * up_ref[...].astype(F32),
                axis=1,
                keepdims=True,
            )
            gg_ref[...] += jnp.broadcast_to(term, gg_ref.shape)


def finish_ffn(pieces, spots, w_gate, w_up, gain):
    n = len(pieces)
    rows, both = pieces[0].shape
    width = both // 2
    block = pl.BlockSpec((rows, width), lambda i, spots: (0, spots[i]))
    return pl.pallas_call(
        functools.partial(finish_ffn_kernel, n),
        grid_spec=pltpu.PrefetchScalarGridSpec(
            num_scalar_prefetch=1,
            grid=(n,),
            in_specs=[pl.BlockSpec((rows, both), lambda i, spots: (0, 0))] * n
            + [block, block, pl.BlockSpec((rows, 1), lambda i, spots: (0, 0))],
            out_specs=[block, block, pl.BlockSpec((rows, 128), lambda i, spots: (0, 0))],
        ),
        out_shape=[
            jax.ShapeDtypeStruct(w_gate.shape, F32),
            jax.ShapeDtypeStruct(w_gate.shape, F32),
            jax.ShapeDtypeStruct((rows, 128), F32),
        ],
        compiler_params=pltpu.CompilerParams(vmem_limit_bytes=24 << 20),
    )(spots, *pieces, w_gate, w_up, gain)


def finish_qkv_kernel(n, spots, pieces, q_ref, k_ref, v_ref, gain_ref, oq, ok, ov, gg_ref):
    q_width = q_ref.shape[1] // n
    sharers = n // KV_HEADS
    gain = gain_ref[...]
    term = jnp.zeros((q_ref.shape[0], 1), F32)
    for kv in range(KV_HEADS):
        held = 0.0
        for j in range(sharers):
            c = kv * sharers + j
            piece = pieces[spots[c]].astype(F32)
            here = slice(c * q_width, (c + 1) * q_width)
            q = piece[:, :q_width]
            held = held + piece[:, q_width:]
            oq[:, here] = q * gain
            term += jnp.sum(q * q_ref[:, here].astype(F32), axis=1, keepdims=True)
        here = slice(kv * HEAD_DIM, (kv + 1) * HEAD_DIM)
        k, v = held[:, :HEAD_DIM], held[:, HEAD_DIM:]
        ok[:, here] = k * gain
        ov[:, here] = v * gain
        term += jnp.sum(
            k * k_ref[:, here].astype(F32) + v * v_ref[:, here].astype(F32), axis=1, keepdims=True
        )
    gg_ref[...] = jnp.broadcast_to(term, gg_ref.shape)


def finish_qkv(pieces, spots, w_query, w_key, w_value, gain):
    n, rows, _ = pieces.shape
    vmem = pl.BlockSpec(memory_space=pltpu.VMEM)
    return pl.pallas_call(
        functools.partial(finish_qkv_kernel, n),
        in_specs=[pl.BlockSpec(memory_space=pltpu.SMEM)] + [vmem] * 5,
        out_specs=[vmem] * 4,
        out_shape=[
            jax.ShapeDtypeStruct(w_query.shape, F32),
            jax.ShapeDtypeStruct(w_key.shape, F32),
            jax.ShapeDtypeStruct(w_value.shape, F32),
            jax.ShapeDtypeStruct((rows, 128), F32),
        ],
    )(spots, pieces, w_query, w_key, w_value, gain)


def norm_back(grad_scaled, unit_rows, inverse):
    return inverse * (
        grad_scaled - unit_rows * jnp.mean(grad_scaled * unit_rows, axis=1, keepdims=True)
    )


def rms_inverse(values):
    return lax.rsqrt(jnp.mean(values * values, axis=1, keepdims=True) + EPSILON)


def body(
    tokens,
    teacher,
    valid_mask,
    lengths,
    span_order,
    w_query,
    w_key,
    w_value,
    w_out,
    w_gate,
    w_up,
    w_down,
    gain_attn,
    gain_ffn,
):
    net = Links()
    n, m, ring = net.n, net.m, net.ring
    x_low = tokens[0]
    tok_rows, width = x_low.shape
    rows = w_query.shape[0]
    heads = HEADS // n
    q_width = heads * HEAD_DIM
    sharers = n // KV_HEADS
    ff_slice = w_gate.shape[1] // n
    stream = tok_rows * n
    spans = tok_rows // SPAN

    jobs, box = net.jobs, net.box

    def later(name, key, job):
        jobs.setdefault(name, {})[key] = job

    def core(x):
        return net.flip(x, "fsdp", 1)

    def side(x):
        return net.flip(x, "fsdp", 2)

    gain_a = gain_attn.astype(F32)[:, None]
    gain_f = gain_ffn.astype(F32)[:, None]
    routes, origins = net.routes(), net.origins()
    pair_moves = [(da, dq) for da in range(ring) for dq in range(2)]
    dests, sources = net.dests(pair_moves), net.sources(pair_moves)
    span_row = jnp.broadcast_to(
        jnp.pad(span_order[0].astype(BF), (0, q_width + 2 * HEAD_DIM - spans))[None, :],
        (16, q_width + 2 * HEAD_DIM),
    )
    straight, across = cut_qkv(n, routes, w_query, w_key, w_value, gain_a, span_row)

    def along(first, other):
        def job(begun):
            ready = tie(jnp.stack([first, box[other]], axis=1), begun)
            return [net.shift(ready[da], da, 0) if da else ready[da] for da in range(ring)]

        return job

    half_rows = w_down.shape[0] // 2
    later("ax0", "q_across", lambda begun: net.shift(across, 0, 1))
    later("ax1", "out_side", lambda begun: side(tie(w_out, begun)))
    later("ax0", "down_side_0", lambda begun: side(w_down[:half_rows]))
    later("ax1", "q_came", along(straight, "q_across"))

    def q_side(begun):
        came = jnp.concatenate(box["q_came"], axis=0)
        return came, side(came)

    later("ax2", "q_sides", q_side)
    later("ax2", "out_core", lambda begun: [core(tie(w_out, begun)), core(box["out_side"])])
    later("ax3", "down_side_1", lambda begun: side(tie(w_down[half_rows:], begun)))
    token_blocks = net.gather_ctx(x_low, "ax")
    q_came, q_other = box["q_sides"]
    qkv_w = net.assemble([[q_came, core(q_came), q_other, core(q_other)]], sources, rows)
    spans_here = tie(q_came, qkv_w)[:, rows, :spans].astype(jnp.int32).reshape(n * spans)
    padding = (-q_width) % 128

    def with_padding(array):
        if not padding:
            return array
        return jnp.concatenate(
            [
                jnp.pad(array[:, :q_width], ((0, 0), (0, padding))),
                array[:, q_width:],
            ],
            axis=1,
        )

    def no_padding(array):
        if not padding:
            return array
        return jnp.concatenate([array[:, :q_width], array[:, q_width + padding :]], axis=1)

    qkv_w = with_padding(qkv_w)
    alone = jnp.zeros((1,), jnp.int32)
    out_w = net.assemble(
        [[x[None] for x in (w_out, box["out_core"][0], box["out_side"], box["out_core"][1])]],
        alone,
        rows,
    )

    direct = net.direct()
    quarter = n // 4
    gate_in, up_in = tie((w_gate, w_up), token_blocks[1][0][0])
    gate_up_cut = cut_ffn(net.dests(direct), gate_in, up_in, gain_f)
    came_ffn = [gate_up_cut[0]]

    def send(pieces, begun, start, stop):
        pieces = tie(pieces, begun)
        return [net.shift(pieces[i], *direct[i]) for i in range(start, stop)]

    place = (
        spans_here[:, None] * SPAN + lax.broadcasted_iota(jnp.int32, (n * spans, SPAN), 1)
    ).reshape(stream)
    seq_ends = jnp.cumsum(lengths[0])
    passed = seq_ends[None, :] <= place[:, None]
    segment = jnp.sum(passed.astype(jnp.int32), axis=1)
    seq_begin = jnp.sum(jnp.where(passed, lengths[0][None, :], 0), axis=1)
    rates = jnp.asarray(rope_rates(HEAD_DIM)[: HEAD_DIM // 2])
    angles = rates[:, None] * (place - seq_begin).astype(F32)[None, :]
    table = jnp.concatenate(
        [
            jnp.cos(angles),
            jnp.sin(angles),
            segment.astype(F32)[None, :],
            place.astype(F32)[None, :],
            jnp.zeros((128 - 66, stream), F32),
        ],
        axis=0,
    )

    x_pairs, inverses, acts_attn = [], [], []
    pair_rows = 2 * tok_rows
    for r in range(ring):
        x_pair = paired(token_blocks[r])
        inverse = rms_inverse(x_pair.astype(F32))
        x_pairs.append(x_pair)
        inverses.append(inverse)
        acts_attn.append(mm(x_pair, qkv_w) * inverse)
    inverse_all = jnp.concatenate(inverses, axis=0)
    act_all = jnp.concatenate(acts_attn, axis=0)
    cuts = [1, max(1, 0 * n // 8), 4 * n // 8, 6 * n // 8, 7 * n // 8, n]
    first = attend(heads, 0, act_all, table)
    sent = send(gate_up_cut, qkv_w, cuts[1], cuts[2])
    act_all, sent = lax.optimization_barrier((act_all, sent))
    came_ffn += sent
    facts = first[4]
    second = attend(heads, 1, act_all, table, facts)
    kv_rot = second[3]
    attended_halves = first[0], second[0]

    def split_pair(block):
        return block[:tok_rows], block[tok_rows:]

    def pair_of(array, r):
        return array[r * pair_rows : (r + 1) * pair_rows]

    inputs = x_low.astype(F32)

    def of_halves(halves, r):
        which, start = divmod(r * pair_rows, stream // 2)
        return halves[which][start : start + pair_rows]

    for i in range(3):
        later(f"ro{i}", f"f_{i}", lambda begun, i=i: send(gate_up_cut, begun, cuts[2 + i], cuts[3 + i]))
    for g in range(4):

        def g_side(begun, g=g):
            pieces = came_ffn + sum((box[f"f_{i}"] for i in range(g)), [])
            block = tie(jnp.stack(pieces[g * quarter : (g + 1) * quarter]), begun)
            return block, side(block)

        def g_core(begun, g=g):
            return [core(x) for x in box[f"g_side{g}"]]

        later(f"ro{g}", f"g_side{g}", g_side)
        later(f"ro{g + 1}" if g < 3 else "ff0", f"g_core{g}", g_core)
    later("ro0", "down_core", lambda begun: core(tie(w_down, begun)))

    def down_far(begun):
        return core(jnp.concatenate([box["down_side_0"], box["down_side_1"]], axis=0))

    later("ff0", "down_far", down_far)
    middle = inputs + net.scatter_ctx(
        lambda r: split_pair(mm(of_halves(attended_halves, r)[:, :q_width], out_w)), "ro"
    )

    inverse_ffn = rms_inverse(middle)
    unit_ffn = middle * inverse_ffn
    unit_blocks = net.gather_ctx(unit_ffn.astype(BF), "ff")
    gate_up_w = net.assemble(
        [
            [box[f"g_side{g}"][0], box[f"g_core{g}"][0], box[f"g_side{g}"][1], box[f"g_core{g}"][1]]
            for g in range(4)
        ],
        net.sources(direct),
        rows,
    )
    down_sides = jnp.concatenate([box["down_side_0"], box["down_side_1"]], axis=0)
    down_w = net.assemble(
        [[x[None] for x in (w_down, box["down_core"], down_sides, box["down_far"])]],
        alone,
        w_down.shape[0],
    )
    z_pairs = [paired(blocks) for blocks in unit_blocks]
    acts, hiddens = {}, {}

    def down_part(r):
        both = mm(z_pairs[r], gate_up_w)
        gate, up = both[:, :ff_slice], both[:, ff_slice:]
        acts[r] = (gate, up)
        hiddens[r] = (gate * jax.nn.sigmoid(gate) * up).astype(BF)
        return split_pair(mm(hiddens[r], down_w))

    out_full = middle + net.scatter_ctx(down_part, "fo")

    valid_f = valid_mask[0].astype(F32)[:, None]
    missed = (out_full - teacher[0].astype(F32)) * valid_f
    sums = jnp.stack([jnp.sum(missed * missed), jnp.sum(valid_f)]).reshape(1, 2)
    grad_out = missed

    grad_blocks = net.gather_ctx(grad_out.astype(BF), "bf")
    grad_pairs = [paired(blocks) for blocks in grad_blocks]
    grad_acts = {}

    def unit_part(r):
        gate, up = acts[r]
        grad_hidden = against(grad_pairs[r], down_w)
        share = jax.nn.sigmoid(gate)
        grad_gate = grad_hidden * up * share * (1.0 + gate * (1.0 - share))
        grad_up = grad_hidden * (gate * share)
        grad_acts[r] = jnp.concatenate([grad_gate.astype(BF), grad_up.astype(BF)], axis=1)
        return split_pair(against(grad_acts[r], gate_up_w))

    owners = net.dests(direct)
    term_slots = ["bo2", "bo3", "am0", "am1", "am2", "am3", "ar0"]

    def listed(items):
        return [items[r] for r in range(ring)]

    for g in range(4):

        def g_term(begun, g=g):
            lefts, rights = tie((z_pairs, listed(grad_acts)), begun)
            return term(m, n, owners[g * quarter : (g + 1) * quarter], net.f, lefts, rights)

        def g_cross(begun, g=g):
            return core(box[f"t{g}"][1])

        def g_far(begun, g=g):
            keep, got = box[f"t{g}"][0], box[f"tc{g}"]
            return side((keep[1].astype(F32) + got[1]).astype(BF))

        later(term_slots[g], f"t{g}", g_term)
        later(term_slots[g + 1], f"tc{g}", g_cross)
        later(term_slots[g + 2], f"ts{g}", g_far)

    def d_term(begun):
        lefts, rights = tie((listed(hiddens), grad_pairs), begun)
        return term(m, 1, alone, net.f, lefts, rights)

    later("am2", "d", d_term)
    later("am3", "dc", lambda begun: core(box["d"][1]))

    def d_far(begun):
        block = (tie(box["d"][0], begun)[1, 0].astype(F32) + box["dc"][1, 0]).astype(BF)
        return block[half_rows:], side(block[:half_rows])


    axes = [("ctx", 1 << i) for i in range((n - 1).bit_length())]
    axes += [("fsdp", 1 << i) for i in range((m - 1).bit_length())]
    spots = [f"am{r}" for r in range(ring)] + [f"ar{r}" for r in range(ring)]
    box["sums"] = sums
    for name, (axis, bit) in zip(spots, axes):
        later(name, "sums", lambda begun, a=axis, b=bit: box["sums"] + net.flip(tie(box["sums"], begun), a, b))

    unit_parts = {r: unit_part(r) for r in net.scatter_order()}
    grad_unit = net.scatter_ctx(unit_parts.get, "bo")
    grad_middle = grad_out + norm_back(grad_unit, unit_ffn, inverse_ffn)
    middle_low = grad_middle.astype(BF)

    middle_blocks = net.gather_ctx(middle_low, "am")
    middle_pairs = [paired(blocks) for blocks in middle_blocks]

    def summed(i):
        g, at = divmod(i, quarter)
        keep, got, far = box[f"t{g}"][0], box[f"tc{g}"], box[f"ts{g}"]
        return (keep[0, at].astype(F32) + got[0, at] + far[at]).astype(BF)

    def send_sum(begun, start, stop):
        return [net.shift(tie(summed(i), begun), *direct[i]) for i in range(start, stop)]

    def back_half(half):
        parts = [
            against(middle_pairs[r], out_w).astype(BF)
            for r in range(half * ring // 2, (half + 1) * ring // 2)
        ]
        grads = jnp.concatenate(parts, axis=0)
        return jnp.pad(grads, ((0, 0), (0, padding))) if padding else grads

    grads_first, grads_second = back_half(0), back_half(1)
    came_sums = [summed(0)]
    cuts = [1, 3 * n // 8, 5 * n // 8, 7 * n // 8, n]
    sent = send_sum(middle_blocks[-1][0][0], cuts[0], cuts[1])
    grads_first, grads_second, sent = lax.optimization_barrier((grads_first, grads_second, sent))
    came_sums += sent
    fixed = kv_rot, table, facts, inverse_all
    sent, box["ds0"] = send_sum(grads_first, cuts[1], cuts[2]), d_far(grads_first)
    backed = attend_back(heads, 0, first[2], grads_first, *fixed, first[1])
    backed, grads_second, sent, box["ds0"] = lax.optimization_barrier(
        (backed, grads_second, sent, box["ds0"])
    )
    came_sums += sent
    gq_first, gs_first, sum_k, sum_v = backed
    sent = send_sum(grads_second, cuts[2], cuts[3])
    box["ds1"] = side(tie(box["ds0"][0], grads_second))
    backed = attend_back(heads, 1, second[2], grads_second, *fixed, second[1], (sum_k, sum_v))
    (gq_second, gs_second, g_kv, gs_kv), sent, box["ds1"] = lax.optimization_barrier(
        (backed, sent, box["ds1"])
    )
    came_sums += sent

    def attn_part(r):
        rows_q = of_halves((gq_first, gq_second), r)
        grads = jnp.concatenate([rows_q, pair_of(g_kv, r)], axis=1)
        return split_pair(against(grads, qkv_w))

    def q_term(begun):
        grads = [
            jnp.concatenate([of_halves((gs_first, gs_second), r), pair_of(gs_kv, r)], axis=1)
            for r in range(ring)
        ]
        lefts, grads = tie((x_pairs, grads), begun)
        return term(m, n, dests, net.f, lefts, grads)

    def q_back(begun):
        (keep, _), got = box["qt"], box["qc"]
        block = keep[0].astype(F32) + got[0] + box["qs"]
        if padding:
            block = jnp.concatenate([block[..., :q_width], block[..., q_width + padding :]], axis=2)
        block = block.astype(BF).reshape(ring, 2, rows, q_width + 2 * HEAD_DIM)
        return block[:, 0], net.shift(block[:, 1], 0, 1)

    def q_along(begun):
        ready = tie(jnp.stack(box["qb"], axis=1), begun)
        return [net.shift(ready[da], da, 0) if da else ready[da] for da in range(ring)]

    def o_term(begun):
        lefts = [of_halves(attended_halves, r)[:, :q_width] for r in range(ring)]
        lefts, grads = tie((lefts, middle_pairs), begun)
        return term(m, 1, alone, net.f, lefts, grads)

    def crossed(key, made):
        return lambda begun: core(tie(box[made][1], begun))

    def farther(made, got):
        return lambda begun: side((box[made][0][1].astype(F32) + box[got][1]).astype(BF))

    def ends(begun):
        square_sum, valid_count = box["sums"][0, 0], box["sums"][0, 1]
        box["loss"] = 0.5 * square_sum / (width * valid_count)
        box["spread"] = (tok_rows * n * m) / valid_count
        pieces = tie(came_sums + box["c_last"], begun)
        return finish_ffn(pieces, net.sources(direct), w_gate, w_up, gain_f * box["spread"])

    later("ar0", "ot", o_term)
    later("ar0", "qt", q_term)
    later("ar0", "c_last", lambda begun: send_sum(begun, cuts[3], n))
    later("ar1", "qc", crossed("qc", "qt"))
    later("ar1", "oc", crossed("oc", "ot"))
    later("ar2", "qs", farther("qt", "qc"))
    later("ar2", "os", farther("ot", "oc"))
    later("ar3", "qb", q_back)
    later(f"ar{max(2, len(axes) - ring)}", "ffn", ends)
    grad_attn = net.scatter_ctx(attn_part, "ar")
    spread = box["spread"]
    inverse_attn = rms_inverse(inputs)
    grad_input = grad_middle + norm_back(grad_attn, inputs * inverse_attn, inverse_attn)
    grad_w_query, grad_w_key, grad_w_value, gain_sum_attn = finish_qkv(
        jnp.concatenate(q_along(grad_attn), axis=0), origins, w_query, w_key, w_value, gain_a * spread
    )
    grad_w_out = (box["ot"][0][0, 0].astype(F32) + box["oc"][0, 0] + box["os"][0]) * spread
    down_keep = box["d"][0][0, 0].astype(F32) + box["dc"][0, 0]
    down_far = jnp.concatenate([box["ds0"][1], box["ds1"]], axis=0)
    grad_down = down_keep + down_far
    grad_w_gate, grad_w_up, gain_sum_ffn = box["ffn"]
    loss_value = box["loss"]
    return (
        out_full.astype(BF)[None],
        loss_value,
        (grad_input * spread)[None],
        grad_w_query,
        grad_w_key,
        grad_w_value,
        grad_w_out,
        grad_w_gate,
        grad_w_up,
        grad_down * spread,
        gain_sum_attn[:, 0] * spread,
        gain_sum_ffn[:, 0] * spread,
    )


def solution(mesh):
    token_spec = P("fsdp", "ctx", None)
    row_spec = P(("ctx", "fsdp"), None)
    gain_spec = P(("ctx", "fsdp"))
    in_specs = (
        token_spec,
        token_spec,
        P("fsdp", "ctx"),
        P("fsdp", None),
        P("fsdp", "ctx"),
        *([row_spec] * 7),
        gain_spec,
        gain_spec,
    )
    out_specs = (token_spec, P(), token_spec, *([row_spec] * 7), gain_spec, gain_spec)
    return jax.shard_map(body, mesh=mesh, in_specs=in_specs, out_specs=out_specs, check_vma=False)
```
